128 devices in a mesh: grp: 8 (over x, core), dev: 16 (over z, y).
Axes of the slice: x: 4, y: 4, z: 4, core: 2. Of those that a mesh axis runs over, the one named last changes fastest.
Arguments:
- points: bfloat16 [65536, 1024], P(('grp', 'dev')), may hold values from -100 to 100
- coarse: int32 [65536, 1], P(('grp', 'dev')), may hold values from 0 to 31; in each aligned block of 512 rows (0 to 511, 512 to 1023, ...) at most 32 rows name the same one
- candidates: int32 [32, 4], replicated, may hold values from 0 to 7, as said below
- centroids: bfloat16 [8192, 1024], P(('grp', 'dev')), may hold values from -0.1875 to 0.1875
Outputs:
- new_centroids: float32 [8192, 1024], P(('grp', 'dev'))
- point_affinity: float32 [65536], P(('grp', 'dev'))
The draws below stay inside these ranges and needn't reach their ends.
Inputs may be any that keep to these rules, and one draw needn't show every extreme that they name: In the rows of one device no coarse cluster is named by more than 32 rows. `candidates`: each row lists 4 different blocks.
All inputs are finite; a program needn't handle non-finite values.
Results may differ from the reference program's by a relative error of at most 0.0045.
Values may be sent and summed in bfloat16 or wider, within the bound.
A program may use at most 64 MiB of HBM per device.

```python
import math
import jax
import jax.numpy as jnp
import numpy as np
from jax import lax

D = 1024
BLK = 128
NBLK = 8
NB = 4
CG = 4
TOK_DEV = 512
K1 = 32
CAP = 32
POINTS = 65536
N_GRP = 8
N_DEV = 16


def draw_points(key, part):
    key = jax.random.fold_in(key, 11)
    first = jax.random.fold_in(key, 0)
    values = jax.random.normal(first, (POINTS, D), jnp.float32)
    values = jnp.clip(values, -6.0, 6.0)
    return values.astype(jnp.bfloat16)


def draw_candidates(key, part):
    key = jax.random.fold_in(key, 23)
    keys = jax.random.split(key, K1)
    orders = jax.vmap(lambda single: jax.random.permutation(single, NBLK))(keys)
    return orders[:, :NB].astype(jnp.int32)


def block_levels(stream_key, dims, cuts, least, largest):
    level = 1.0
    for position, parts in cuts:
        heights = jax.random.uniform(jax.random.fold_in(jax.random.fold_in(stream_key, 6), position), (parts,), jnp.float32, least / len(cuts), largest / len(cuts))
        level = level * jnp.repeat(jnp.exp(heights), dims[position] // parts).reshape((-1,) + (1,) * (len(dims) - 1 - position))
    return level


def assign_block(stream_key, own, number, rows, count, top, reach, lean):
    order = jax.random.permutation(stream_key, count)
    crowded, ordinary = shares(count, rows * top, reach, lean, True), shares(count, rows * top, reach, lean, False)
    places = jnp.arange(count)

    def named(sizes, turn):
        used = int((sizes > 0).sum())
        fixed = max(1, used // 4)
        moved = fixed + (places - fixed + turn * (used - fixed)) % max(1, count - fixed)
        return jnp.zeros((count,), jnp.int32).at[order[jnp.where(places < fixed, places, moved)]].set(jnp.asarray(sizes, jnp.int32))

    sizes = jnp.where(number % 4 == 0, named(crowded, number // 4), named(ordinary, number - number // 4 - 1))
    mixed = jax.random.permutation(jax.random.fold_in(own, 3), count)
    donor, taker = mixed[0:count // 2 * 2:2], mixed[1:count // 2 * 2:2]
    slack = jnp.minimum(sizes[donor] - 1, reach - sizes[taker]) // 2
    slack = jnp.where((donor == order[0]) | (taker == order[0]) | (sizes[taker] == 0), 0, jnp.maximum(slack, 0))
    moved = jax.random.randint(jax.random.fold_in(own, 4), (count // 2,), 0, 1 << 20) % (slack + 1)
    sizes = sizes.at[donor].add(-moved).at[taker].add(moved)
    items = jnp.searchsorted(jnp.cumsum(sizes), jnp.arange(rows * top), side="right").astype(jnp.int32)
    grid = items.reshape(top, rows).T
    grid = grid[jax.random.permutation(jax.random.fold_in(own, 1), rows)]
    turn = jax.random.randint(jax.random.fold_in(own, 2), (rows, 1), 0, top)
    return jnp.take_along_axis(grid, (jnp.arange(top)[None, :] + turn) % top, axis=1)


def shares(number_of, total, bound, slope, full):
    loads = [(1 << 20) // math.isqrt(rank ** slope) + 1 for rank in range(1, number_of + 1)]
    largest = bound if full else min(bound, max(-(-total // number_of), total * loads[0] // sum(loads)))
    least = 1 if total - largest >= number_of - 1 else 0
    holding, rest = [largest] + [least] * (number_of - 1), total - largest - least * (number_of - 1)
    while rest > 0:
        free = [i for i in range(1, number_of) if holding[i] < largest] or [i for i in range(1, number_of) if holding[i] < bound]
        whole, budget = sum([loads[i] for i in free]), rest
        for i in free:
            more = min(bound - holding[i], max(1, budget * loads[i] // whole), rest)
            holding[i] = holding[i] + more
            rest = rest - more
    return np.array(holding)


def gaussian(key, shape, scale, limit, shards=(), held_as=jnp.bfloat16):
    entries = jax.random.normal(key, shape, jnp.float32) * scale
    if len(shards) > 0:
        entries = block_levels(key, shape, shards, -0.22, 0.18) * entries
    return jnp.clip(entries, min=-limit, max=limit).astype(held_as)


def setup_inputs(seed: int = 0) -> dict:
    streams_of = jax.random.split(jax.random.key(seed), 5)
    points = draw_points(jax.random.fold_in(streams_of[4], 71), 0)
    coarse_keys = jax.random.split(jax.random.fold_in(streams_of[1], 1), POINTS // TOK_DEV)
    coarse_turns = jax.random.permutation(jax.random.fold_in(streams_of[1], 3), POINTS // TOK_DEV)
    coarse = jax.vmap(lambda own, number: assign_block(jax.random.fold_in(streams_of[1], 2), own, number, TOK_DEV, K1, 1, CAP, 2))(coarse_keys, coarse_turns).reshape((POINTS, 1))
    candidates = draw_candidates(jax.random.fold_in(streams_of[4], 71), 0)
    centroids = gaussian(streams_of[3], (N_GRP * NBLK * BLK, D), D ** -0.5, 0.1875, ((0, 128),))
    return {"points": points, "coarse": coarse, "candidates": candidates, "centroids": centroids}


SOFTMAX_TEMP = 0.4
PRIOR_WEIGHT = 1.0


def reference(points, coarse, candidates, centroids):
    sources = N_GRP * N_DEV
    label = coarse[:, 0].reshape(sources, TOK_DEV)
    onehot = (label[:, :, None] == jnp.arange(K1, dtype=jnp.int32)[None, None, :]).astype(jnp.int32)
    ranking = jnp.sum((jnp.cumsum(onehot, axis=1) - onehot) * onehot, axis=2)
    column = jnp.arange(sources, dtype=jnp.int32)[:, None] * CAP + ranking
    point_ids = jnp.arange(POINTS, dtype=jnp.int32).reshape(sources, TOK_DEV)
    table = jnp.zeros((K1, sources * CAP), jnp.int32).at[label, column].set(point_ids)
    present = jnp.zeros((K1, sources * CAP), jnp.float32).at[label, column].set(1.0)
    blocked = centroids.reshape(N_GRP * NBLK, BLK, D)

    def visit(carry, cluster):
        sums, totals = carry
        chosen = (candidates[cluster] + (cluster // CG) * NBLK).astype(jnp.int32)
        member_rows = blocked[chosen].reshape(NB * BLK, D).astype(jnp.float32)
        centroid_norms = jnp.sum(member_rows * member_rows, axis=1)
        rows = points[table[cluster]].astype(jnp.float32)
        inner_products = jnp.dot(rows, member_rows.T, precision=lax.Precision.HIGHEST)
        logit_scores = (2.0 * inner_products - centroid_norms[None, :]) / SOFTMAX_TEMP
        top_logit = jnp.max(logit_scores, axis=1, keepdims=True)
        exponent_values = jnp.exp(logit_scores - top_logit)
        total_sum = jnp.sum(exponent_values, axis=1, keepdims=True)
        probs = exponent_values / total_sum
        cluster_affinity = SOFTMAX_TEMP * (top_logit[:, 0] + jnp.log(total_sum[:, 0]))
        weights = lax.optimization_barrier((probs * present[cluster][:, None]).astype(jnp.bfloat16))
        weights = weights.astype(jnp.float32)
        part = jnp.dot(weights.T, rows, precision=lax.Precision.HIGHEST)
        sums = sums.at[chosen].add(part.reshape(NB, BLK, D))
        totals = totals.at[chosen].add(jnp.sum(weights, axis=0).reshape(NB, BLK))
        return (sums, totals), cluster_affinity

    start = (jnp.zeros((N_GRP * NBLK, BLK, D), jnp.float32), jnp.zeros((N_GRP * NBLK, BLK), jnp.float32))
    (sums, totals), affinities = lax.scan(visit, start, jnp.arange(K1, dtype=jnp.int32))
    updated = (sums.reshape(-1, D) + PRIOR_WEIGHT * centroids.astype(jnp.float32)) / (totals.reshape(-1) + PRIOR_WEIGHT)[:, None]
    point_affinity = affinities[label, column].reshape(POINTS)
    return updated, point_affinity
```

```python
import functools

import jax
import jax.numpy as jnp
from jax import lax
from jax.experimental import pallas as pl
from jax.experimental.pallas import tpu as pltpu
from jax.sharding import PartitionSpec as P

MESH = pl.DeviceIdType.MESH
F32 = jnp.float32
BF16 = jnp.bfloat16

SOFTMAX_TEMP = 0.4
PRIOR_WEIGHT = 1.0
FAR = 1e30

GROUPS = 8
MEMBERS = 16
ROWS = 512
WIDTH = 1024
SHARD = 64
POOL = MEMBERS * SHARD
PER_GROUP = 4
CLUSTERS = 32
CAP = 32
LISTED = 4
BLK = 128
SLOTS = PER_GROUP * CAP
HALF = WIDTH // 2
QUARTER = WIDTH // 4


def iota(shape, axis):
    return lax.broadcasted_iota(jnp.int32, shape, axis)


def kernel(
    cand,
    points,
    coarse,
    cent,
    new_ref,
    aff_ref,
    tx,
    rx,
    txf,
    rxf,
    pool,
    norms,
    logits,
    weights,
    afftx,
    affrx,
    tottx,
    totrx,
    part_a,
    part_b,
    own_a,
    own_b,
    far1_a,
    near1_a,
    far1_b,
    near1_b,
    send2_a,
    send2_b,
    far2_a,
    near2_a,
    far2_b,
    near2_b,
    local_sem,
    row_send,
    row_recv,
    flag_send,
    flag_recv,
    aff_send,
    aff_recv,
    tot_send,
    tot_recv,
    ag1_send,
    ag1_recv,
    ag2_send,
    ag2_recv,
    far_send,
    far_recv,
    near_send,
    near_recv,
):
    g = lax.axis_index("grp")
    d = lax.axis_index("dev")
    x, c = lax.div(g, 2), lax.rem(g, 2)
    z, y = lax.div(d, 4), lax.rem(d, 4)

    def group_at(k):
        return lax.rem(x + k // 2, 4) * 2 + lax.rem(c + k % 2, 2)

    def group_from(k):
        return lax.rem(x + 4 - k // 2, 4) * 2 + lax.rem(c + k % 2, 2)

    def turn(value, by):
        return lax.rem(value + by + 4, 4)

    def member(first, second, axis):
        return first * 4 + second if axis == 0 else second * 4 + first

    place = ((z, y), (y, z))

    barrier = pltpu.get_barrier_semaphore()
    for k in range(1, GROUPS):
        pl.semaphore_signal(barrier, inc=1, device_id=(group_at(k), d), device_id_type=MESH)
    for k in range(1, MEMBERS):
        pl.semaphore_signal(
            barrier, inc=1, device_id=(g, lax.rem(d + k, MEMBERS)), device_id_type=MESH
        )

    own_copy = pltpu.make_async_copy(cent, pool.at[d], local_sem)
    own_copy.start()
    cluster_ids = iota((CLUSTERS, ROWS), 0)
    named = (coarse[...] == cluster_ids).astype(F32)
    before = (iota((ROWS, ROWS), 0) < iota((ROWS, ROWS), 1)).astype(F32).astype(BF16)
    rank = jnp.dot(named.astype(BF16), before, preferred_element_type=F32)
    slot = jnp.sum(named * (rank + (cluster_ids * CAP).astype(F32)), axis=0, keepdims=True)
    count = jnp.sum(named, axis=1, keepdims=True)
    slot_ids = iota((SLOTS, ROWS), 0)
    lane = iota((CLUSTERS, SLOTS), 1)
    lane_cluster, lane_rank = lax.div(lane, CAP), lax.rem(lane, CAP)

    def pack(k, owner, rows_ref, flag_ref):
        here = slot == (slot_ids + owner * SLOTS).astype(F32)
        rows_ref[k] = jnp.dot(
            here.astype(F32).astype(BF16), points[...], preferred_element_type=F32
        ).astype(BF16)
        mine = iota((CLUSTERS, SLOTS), 0) == lane_cluster + owner * PER_GROUP
        held = jnp.sum(jnp.where(mine, count, 0.0), axis=0, keepdims=True)
        live = (lane_rank[0:1].astype(F32) < held).astype(F32)
        flag_ref[k] = jnp.broadcast_to(live, (8, SLOTS))

    def row_copy(k):
        return pltpu.make_async_remote_copy(
            src_ref=tx.at[k],
            dst_ref=rx.at[k],
            send_sem=row_send.at[k],
            recv_sem=row_recv.at[k],
            device_id=(group_at(k), d),
            device_id_type=MESH,
        )

    def flag_copy(k):
        return pltpu.make_async_remote_copy(
            src_ref=txf.at[k],
            dst_ref=rxf.at[k],
            send_sem=flag_send.at[k],
            recv_sem=flag_recv.at[k],
            device_id=(group_at(k), d),
            device_id_type=MESH,
        )

    def columns(axis):
        return pl.ds(axis * HALF, HALF)

    def gather1(axis, k):
        first, second = place[axis]
        piece = pool.at[d, :, columns(axis)]
        return pltpu.make_async_remote_copy(
            src_ref=piece,
            dst_ref=piece,
            send_sem=ag1_send.at[axis, k],
            recv_sem=ag1_recv.at[axis, k],
            device_id=(g, member(turn(first, k), second, axis)),
            device_id_type=MESH,
        )

    def gather2(axis, k1, k2):
        first, second = place[axis]
        piece = pool.at[member(turn(first, -k1), second, axis), :, columns(axis)]
        return pltpu.make_async_remote_copy(
            src_ref=piece,
            dst_ref=piece,
            send_sem=ag2_send.at[axis, k1, k2],
            recv_sem=ag2_recv.at[axis, k1, k2],
            device_id=(g, member(first, turn(second, k2), axis)),
            device_id_type=MESH,
        )

    own_copy.wait()
    pl.semaphore_wait(barrier, GROUPS - 1 + MEMBERS - 1)
    for axis in (0, 1):
        for k in (2, 1, 3):
            gather1(axis, k).start()
    for k in (4, 5, 2, 6, 3, 7, 1):
        pack(k, group_at(k), tx, txf)
        flag_copy(k).start()
        row_copy(k).start()
        if k == 2:
            for axis in (0, 1):
                for k2 in (2, 1, 3):
                    gather2(axis, 0, k2).start()
    pack(0, g, rx, rxf)

    for k1 in (1, 3, 2):
        for axis in (0, 1):
            gather1(axis, k1).wait_recv()
            for k2 in (2, 1, 3):
                gather2(axis, k1, k2).start()

    block = iota((8, SLOTS), 0)
    allowed = jnp.zeros((8, SLOTS), jnp.bool_)
    wide_cluster = lax.div(iota((8, SLOTS), 1), CAP)
    for cluster in range(PER_GROUP):
        for j in range(LISTED):
            listed = cand[j, g * PER_GROUP + cluster]
            allowed = allowed | ((block == listed) & (wide_cluster == cluster))
    penalty = jnp.where(allowed, 0.0, FAR)

    for axis in (0, 1):
        for k1 in range(4):
            for k2 in range(1, 4):
                gather2(axis, k1, k2).wait_recv()

    for b in range(8):
        rows = pool[2 * b : 2 * b + 2].reshape(BLK, WIDTH).astype(F32)
        square = jnp.sum(rows * rows, axis=1, keepdims=True)
        norms[b] = square + penalty[b : b + 1]

    def aff_copy(k):
        return pltpu.make_async_remote_copy(
            src_ref=afftx.at[k],
            dst_ref=affrx.at[k],
            send_sem=aff_send.at[k],
            recv_sem=aff_recv.at[k],
            device_id=(group_from(k), d),
            device_id_type=MESH,
        )

    def score(pair):
        for k in (2 * pair, 2 * pair + 1):
            if k:
                flag_copy(k).wait_recv()
                row_copy(k).wait_recv()
        rows = rx[2 * pair : 2 * pair + 2].reshape(2 * SLOTS, WIDTH)
        live = jnp.concatenate([rxf[2 * pair, 0:1], rxf[2 * pair + 1, 0:1]], axis=1)

        def first(t, top):
            tile = pool[pl.ds(4 * t, 4)].reshape(4 * SHARD, WIDTH)
            inner = lax.dot_general(
                tile, rows, (((1,), (1,)), ((), ())), preferred_element_type=F32
            )
            square = norms[pl.ds(2 * t, 2)].reshape(4 * SHARD, SLOTS)
            value = (2.0 * inner - jnp.concatenate([square, square], axis=1)) * (
                1.0 / SOFTMAX_TEMP
            )
            logits[t] = value
            return jnp.maximum(top, jnp.max(value, axis=0, keepdims=True))

        top = lax.fori_loop(0, 4, first, jnp.full((1, 2 * SLOTS), -jnp.inf, F32))

        def second(t, total):
            value = jnp.exp(logits[t] - top)
            logits[t] = value
            return total + jnp.sum(value, axis=0, keepdims=True)

        total = lax.fori_loop(0, 4, second, jnp.zeros((1, 2 * SLOTS), F32))
        scale = live / total

        def third(t, carry):
            weights[pl.ds(4 * t, 4), :, pl.ds(2 * pair * SLOTS, 2 * SLOTS)] = (
                (logits[t] * scale).astype(BF16).reshape(4, SHARD, 2 * SLOTS)
            )
            return carry

        lax.fori_loop(0, 4, third, 0)
        affinity = SOFTMAX_TEMP * (top + jnp.log(total))
        for i, k in enumerate((2 * pair, 2 * pair + 1)):
            mine = jnp.broadcast_to(affinity[:, i * SLOTS : (i + 1) * SLOTS], (8, SLOTS))
            if k:
                afftx[k] = mine
                aff_copy(k).start()
            else:
                affrx[0] = mine

    for pair in (0, 1, 3, 2):
        score(pair)

    part = (part_a, part_b)
    own = (own_a, own_b)
    far1, near1 = (far1_a, far1_b), (near1_a, near1_b)
    send2 = (send2_a, send2_b)
    far2, near2 = (far2_a, far2_b), (near2_a, near2_b)

    def product(axis, index):
        if axis == 0:
            lhs = weights[pl.ds(4 * index, 4)].reshape(4 * SHARD, POOL)
        else:
            lhs = jnp.concatenate([weights[4 * i + index] for i in range(4)], axis=0)
        rhs = rx[:, :, axis * HALF : (axis + 1) * HALF].reshape(GROUPS * SLOTS, HALF)
        return jnp.dot(lhs, rhs, preferred_element_type=F32)

    def hop(phase, axis, side, near, part_index):
        first, second = place[axis]
        step = 1 - 2 * side
        if phase == 0:
            target = member(turn(first, step), second, axis)
            source = part[axis].at[turn(first, step if near else 2)]
        else:
            target = member(first, turn(second, step), axis)
            source = send2[axis].at[turn(second, step if near else 2)]
        piece = pl.ds(part_index * QUARTER, QUARTER)
        if near:
            landing = (near1, near2)[phase][axis].at[side, :, piece]
            semaphores = near_send.at[phase, axis, side, part_index], near_recv.at[
                phase, axis, side, part_index
            ]
        else:
            landing = (far1, far2)[phase][axis].at[side]
            semaphores = far_send.at[phase, axis, side], far_recv.at[phase, axis, side]
        return pltpu.make_async_remote_copy(
            src_ref=source.at[:, piece],
            dst_ref=landing,
            send_sem=semaphores[0],
            recv_sem=semaphores[1],
            device_id=(g, target),
            device_id_type=MESH,
        )

    def add_far(phase, axis, side):
        first, second = place[axis]
        buffer = (part, send2)[phase][axis]
        landing = (far1, far2)[phase][axis]
        index = turn((first, second)[phase], 1 - 2 * side)
        hop(phase, axis, side, False, side).wait_recv()
        piece = slice(side * QUARTER, (side + 1) * QUARTER)
        buffer[index, :, piece] = (
            buffer[index, :, piece].astype(F32) + landing[side].astype(F32)
        ).astype(BF16)
        hop(phase, axis, side, True, side).start()

    for axis in (0, 1):
        index = turn(place[axis][0], 2)
        part[axis][index] = product(axis, index).astype(BF16)
        for side in (0, 1):
            hop(0, axis, side, False, side).start()
    for axis in (0, 1):
        for side in (0, 1):
            index = turn(place[axis][0], 1 - 2 * side)
            part[axis][index] = product(axis, index).astype(BF16)
            hop(0, axis, side, True, 1 - side).start()

    lanes = iota((SHARD, BLK), 1)
    diagonal = lanes == iota((SHARD, BLK), 0)

    def total_copy(k):
        return pltpu.make_async_remote_copy(
            src_ref=tottx.at[lax.rem(d + k, MEMBERS)],
            dst_ref=totrx.at[k],
            send_sem=tot_send.at[k],
            recv_sem=tot_recv.at[k],
            device_id=(g, lax.rem(d + k, MEMBERS)),
            device_id_type=MESH,
        )

    def total_of(i, carry):
        column = jnp.sum(weights[i].astype(F32), axis=1, keepdims=True)
        row = jnp.sum(jnp.where(diagonal, column, 0.0), axis=0, keepdims=True)
        tottx[i] = jnp.broadcast_to(row, (8, BLK))
        return carry

    lax.fori_loop(0, MEMBERS, total_of, 0)
    for k in range(1, MEMBERS):
        total_copy(k).start()

    for axis in (0, 1):
        for side in (0, 1):
            add_far(0, axis, side)
    for axis in (0, 1):
        own[axis][...] = product(axis, place[axis][0])

    affinity = jnp.zeros((1, ROWS), F32)
    square_eye = iota((SLOTS, SLOTS), 0) == iota((SLOTS, SLOTS), 1)
    for k in range(GROUPS):
        if k:
            aff_copy(k).wait_recv()
        column = jnp.sum(jnp.where(square_eye, affrx[k, 0:1], 0.0), axis=1, keepdims=True)
        here = slot == (slot_ids + group_at(k) * SLOTS).astype(F32)
        affinity = affinity + jnp.sum(jnp.where(here, column, 0.0), axis=0, keepdims=True)
    aff_ref[...] = affinity

    for axis in (0, 1):
        total = own[axis][...]
        for side in (0, 1):
            for piece in (0, 1):
                hop(0, axis, side, True, piece).wait_recv()
            total = total + near1[axis][side].astype(F32)
        own[axis][...] = total
        send2[axis][...] = total.astype(BF16).reshape(4, SHARD, HALF)
        for side in (0, 1):
            hop(1, axis, side, False, side).start()
        for side in (0, 1):
            hop(1, axis, side, True, 1 - side).start()
    for axis in (0, 1):
        for side in (0, 1):
            add_far(1, axis, side)

    totals = tottx[d]
    for k in range(1, MEMBERS):
        total_copy(k).wait_recv()
        totals = totals + totrx[k]
    column = jnp.sum(jnp.where(diagonal, totals[0:1], 0.0), axis=1, keepdims=True)

    for axis in (0, 1):
        mine = own[axis][pl.ds(place[axis][1] * SHARD, SHARD)]
        for side in (0, 1):
            for piece in (0, 1):
                hop(1, axis, side, True, piece).wait_recv()
            mine = mine + near2[axis][side].astype(F32)
        span = slice(axis * HALF, (axis + 1) * HALF)
        new_ref[:, span] = (mine + PRIOR_WEIGHT * cent[:, span].astype(F32)) / (
            column + PRIOR_WEIGHT
        )

    for k in range(1, GROUPS):
        flag_copy(k).wait_send()
        row_copy(k).wait_send()
        aff_copy(k).wait_send()
    for k in range(1, MEMBERS):
        total_copy(k).wait_send()
    for axis in (0, 1):
        for k in range(1, 4):
            gather1(axis, k).wait_send()
            for k1 in range(4):
                gather2(axis, k1, k).wait_send()
        for phase in (0, 1):
            for side in (0, 1):
                hop(phase, axis, side, False, side).wait_send()
                for piece in (0, 1):
                    hop(phase, axis, side, True, piece).wait_send()


def local(points, coarse, candidates, centroids):
    vmem = pl.BlockSpec(memory_space=pltpu.VMEM)
    dma = pltpu.SemaphoreType.DMA
    updated, affinity = pl.pallas_call(
        kernel,
        out_shape=(
            jax.ShapeDtypeStruct((SHARD, WIDTH), F32),
            jax.ShapeDtypeStruct((1, ROWS), F32),
        ),
        in_specs=[pl.BlockSpec(memory_space=pltpu.SMEM), vmem, vmem, vmem],
        out_specs=(vmem, vmem),
        scratch_shapes=[
            pltpu.VMEM((GROUPS, SLOTS, WIDTH), BF16),
            pltpu.VMEM((GROUPS, SLOTS, WIDTH), BF16),
            pltpu.VMEM((GROUPS, 8, SLOTS), F32),
            pltpu.VMEM((GROUPS, 8, SLOTS), F32),
            pltpu.VMEM((MEMBERS, SHARD, WIDTH), BF16),
            pltpu.VMEM((8, BLK, SLOTS), F32),
            pltpu.VMEM((4, 4 * SHARD, 2 * SLOTS), F32),
            pltpu.VMEM((MEMBERS, SHARD, GROUPS * SLOTS), BF16),
            pltpu.VMEM((GROUPS, 8, SLOTS), F32),
            pltpu.VMEM((GROUPS, 8, SLOTS), F32),
            pltpu.VMEM((MEMBERS, 8, BLK), F32),
            pltpu.VMEM((MEMBERS, 8, BLK), F32),
            pltpu.VMEM((4, 4 * SHARD, HALF), BF16),
            pltpu.VMEM((4, 4 * SHARD, HALF), BF16),
            pltpu.VMEM((4 * SHARD, HALF), F32),
            pltpu.VMEM((4 * SHARD, HALF), F32),
            pltpu.VMEM((2, 4 * SHARD, QUARTER), BF16),
            pltpu.VMEM((2, 4 * SHARD, HALF), BF16),
            pltpu.VMEM((2, 4 * SHARD, QUARTER), BF16),
            pltpu.VMEM((2, 4 * SHARD, HALF), BF16),
            pltpu.VMEM((4, SHARD, HALF), BF16),
            pltpu.VMEM((4, SHARD, HALF), BF16),
            pltpu.VMEM((2, SHARD, QUARTER), BF16),
            pltpu.VMEM((2, SHARD, HALF), BF16),
            pltpu.VMEM((2, SHARD, QUARTER), BF16),
            pltpu.VMEM((2, SHARD, HALF), BF16),
            dma,
            dma((GROUPS,)),
            dma((GROUPS,)),
            dma((GROUPS,)),
            dma((GROUPS,)),
            dma((GROUPS,)),
            dma((GROUPS,)),
            dma((MEMBERS,)),
            dma((MEMBERS,)),
            dma((2, 4)),
            dma((2, 4)),
            dma((2, 4, 4)),
            dma((2, 4, 4)),
            dma((2, 2, 2)),
            dma((2, 2, 2)),
            dma((2, 2, 2, 2)),
            dma((2, 2, 2, 2)),
        ],
        compiler_params=pltpu.CompilerParams(
            collective_id=0, has_side_effects=True, vmem_limit_bytes=40 << 20
        ),
    )(candidates.T, points, coarse.reshape(1, ROWS), centroids)
    return updated, affinity.reshape(ROWS)


def solution(mesh):
    return jax.shard_map(
        local,
        mesh=mesh,
        in_specs=(P(("grp", "dev"), None), P(("grp", "dev"), None), P(), P(("grp", "dev"), None)),
        out_specs=(P(("grp", "dev"), None), P(("grp", "dev"))),
        check_vma=False,
    )
```

```python
import jax
import jax.numpy as jnp
from jax import lax
from jax.experimental import pallas as pl
from jax.experimental.pallas import tpu as pltpu
from jax.sharding import PartitionSpec as P

MESH = pl.DeviceIdType.MESH
F32 = jnp.float32
BF16 = jnp.bfloat16

SOFTMAX_TEMP = 0.4
PRIOR_WEIGHT = 1.0
FAR = 1e30

GROUPS = 8
MEMBERS = 16
ROWS = 512
WIDTH = 1024
SHARD = 64
POOL = MEMBERS * SHARD
PER_GROUP = 4
CLUSTERS = 32
CAP = 32
LISTED = 4
BLK = 128
SLOTS = PER_GROUP * CAP
HALF = WIDTH // 2
QUARTER = WIDTH // 4
SUBS = 2
SUB = SHARD // SUBS
ORDER = (4, 5, 2, 6, 3, 7, 1)
PAIRS = ((0, 1), (4, 5), (2, 6), (3, 7))


def iota(shape, axis):
    return lax.broadcasted_iota(jnp.int32, shape, axis)


def kernel(
    cand_hbm,
    points_hbm,
    coarse_hbm,
    cent_hbm,
    new_ref,
    aff_ref,
    cand,
    points,
    coarse,
    tx,
    rx,
    txf,
    rxf,
    pool,
    norms,
    logits,
    weights,
    afftx,
    affrx,
    tot1,
    tot1rx,
    tot2,
    tot2rx,
    part_a,
    part_b,
    own_a,
    own_b,
    far_a,
    far_b,
    near_a,
    near_b,
    send_a,
    send_b,
    last_a,
    last_b,
    in_sem,
    row_send,
    row_recv,
    flag_send,
    flag_recv,
    aff_send,
    aff_recv,
    tot_send,
    tot_recv,
    ag1_send,
    ag1_recv,
    ag2_send,
    ag2_recv,
    far_send,
    far_recv,
    near_send,
    near_recv,
    last_send,
    last_recv,
):
    g = lax.axis_index("grp")
    d = lax.axis_index("dev")
    x, c = lax.div(g, 2), lax.rem(g, 2)
    z, y = lax.div(d, 4), lax.rem(d, 4)

    def group_at(k):
        return lax.rem(x + k // 2, 4) * 2 + lax.rem(c + k % 2, 2)

    def group_from(k):
        return lax.rem(x + 4 - k // 2, 4) * 2 + lax.rem(c + k % 2, 2)

    def turn(value, by):
        return lax.rem(value + by + 4, 4)

    def member(first, second, axis):
        return first * 4 + second if axis == 0 else second * 4 + first

    place = ((z, y), (y, z))

    def remote(src, dst, send_sem, recv_sem, device):
        return pltpu.make_async_remote_copy(
            src_ref=src,
            dst_ref=dst,
            send_sem=send_sem,
            recv_sem=recv_sem,
            device_id=device,
            device_id_type=MESH,
        )

    barrier = pltpu.get_barrier_semaphore()
    for k in range(1, GROUPS):
        pl.semaphore_signal(barrier, inc=1, device_id=(group_at(k), d), device_id_type=MESH)
    for axis in (0, 1):
        first, second = place[axis]
        for k in range(1, 4):
            pl.semaphore_signal(
                barrier,
                inc=1,
                device_id=(g, member(turn(first, k), second, axis)),
                device_id_type=MESH,
            )

    coarse_in = pltpu.make_async_copy(coarse_hbm, coarse, in_sem.at[0])
    points_in = pltpu.make_async_copy(points_hbm, points, in_sem.at[1])
    cent_in = pltpu.make_async_copy(cent_hbm, pool.at[d], in_sem.at[2])
    cand_in = pltpu.make_async_copy(cand_hbm, cand, in_sem.at[3])
    coarse_in.start()
    points_in.start()
    cent_in.start()
    cand_in.start()

    cluster_ids = iota((CLUSTERS, ROWS), 0)
    before = (iota((ROWS, ROWS), 0) < iota((ROWS, ROWS), 1)).astype(F32).astype(BF16)
    coarse_in.wait()
    named = (coarse[...] == cluster_ids).astype(F32)
    rank = jnp.dot(named.astype(BF16), before, preferred_element_type=F32)
    slot = jnp.sum(named * (rank + (cluster_ids * CAP).astype(F32)), axis=0, keepdims=True)
    count = jnp.sum(named, axis=1, keepdims=True)
    slot_ids = iota((SLOTS, ROWS), 0)
    lane = iota((CLUSTERS, SLOTS), 1)
    lane_cluster, lane_rank = lax.div(lane, CAP), lax.rem(lane, CAP)

    def pack(k, owner, rows_ref, flag_ref):
        here = slot == (slot_ids + owner * SLOTS).astype(F32)
        rows_ref[k] = jnp.dot(
            here.astype(F32).astype(BF16), points[...], preferred_element_type=F32
        ).astype(BF16)
        mine = iota((CLUSTERS, SLOTS), 0) == lane_cluster + owner * PER_GROUP
        held = jnp.sum(jnp.where(mine, count, 0.0), axis=0, keepdims=True)
        live = (lane_rank[0:1].astype(F32) < held).astype(F32)
        flag_ref[k] = jnp.broadcast_to(live, (8, SLOTS))

    def row_copy(k):
        return remote(tx.at[k], rx.at[k], row_send.at[k], row_recv.at[k], (group_at(k), d))

    def flag_copy(k):
        return remote(txf.at[k], rxf.at[k], flag_send.at[k], flag_recv.at[k], (group_at(k), d))

    def aff_copy(k):
        return remote(afftx.at[k], affrx.at[k], aff_send.at[k], aff_recv.at[k], (group_from(k), d))

    def columns(axis):
        return pl.ds(axis * HALF, HALF)

    def gather1(axis, k):
        first, second = place[axis]
        piece = pool.at[d, :, columns(axis)]
        return remote(
            piece,
            piece,
            ag1_send.at[axis, k],
            ag1_recv.at[axis, k],
            (g, member(turn(first, k), second, axis)),
        )

    def gather2(axis, k1, k2):
        first, second = place[axis]
        piece = pool.at[member(turn(first, -k1), second, axis), :, columns(axis)]
        return remote(
            piece,
            piece,
            ag2_send.at[axis, k1, k2],
            ag2_recv.at[axis, k1, k2],
            (g, member(first, turn(second, k2), axis)),
        )

    points_in.wait()
    for k in ORDER[:2]:
        pack(k, group_at(k), tx, txf)
    cent_in.wait()
    pl.semaphore_wait(barrier, GROUPS - 1 + 6)
    for axis in (0, 1):
        for k in (2, 1, 3):
            gather1(axis, k).start()
    for i, k in enumerate(ORDER):
        if i >= 2:
            pack(k, group_at(k), tx, txf)
        row_copy(k).start()
        flag_copy(k).start()
        if i == 1:
            for axis in (0, 1):
                for k2 in (2, 1, 3):
                    gather2(axis, 0, k2).start()
    pack(0, g, rx, rxf)

    for k1 in (1, 3, 2):
        for axis in (0, 1):
            gather1(axis, k1).wait_recv()
            for k2 in (2, 1, 3):
                gather2(axis, k1, k2).start()

    cand_in.wait()
    block = iota((8, SLOTS), 0)
    allowed = jnp.zeros((8, SLOTS), jnp.bool_)
    wide_cluster = lax.div(iota((8, SLOTS), 1), CAP)
    for cluster in range(PER_GROUP):
        for j in range(LISTED):
            listed = cand[j, g * PER_GROUP + cluster]
            allowed = allowed | ((block == listed) & (wide_cluster == cluster))
    penalty = jnp.where(allowed, 0.0, FAR)

    for axis in (0, 1):
        for k1 in range(4):
            for k2 in range(1, 4):
                gather2(axis, k1, k2).wait_recv()

    for b in range(8):
        rows = pool[2 * b : 2 * b + 2].reshape(BLK, WIDTH).astype(F32)
        square = jnp.sum(rows * rows, axis=1, keepdims=True)
        norms[b] = square + penalty[b : b + 1]

    def score(number, pair):
        for k in pair:
            if k:
                row_copy(k).wait_recv()
                flag_copy(k).wait_recv()
        rows = jnp.concatenate([rx[k] for k in pair], axis=0)
        live = jnp.concatenate([rxf[k, 0:1] for k in pair], axis=1)

        def first(t, top):
            tile = pool[pl.ds(4 * t, 4)].reshape(4 * SHARD, WIDTH)
            inner = lax.dot_general(
                tile, rows, (((1,), (1,)), ((), ())), preferred_element_type=F32
            )
            square = norms[pl.ds(2 * t, 2)].reshape(4 * SHARD, SLOTS)
            value = (2.0 * inner - jnp.concatenate([square, square], axis=1)) * (
                1.0 / SOFTMAX_TEMP
            )
            logits[t] = value
            return jnp.maximum(top, jnp.max(value, axis=0, keepdims=True))

        top = lax.fori_loop(0, 4, first, jnp.full((1, 2 * SLOTS), -jnp.inf, F32))

        def second(t, total):
            value = jnp.exp(logits[t] - top)
            logits[t] = value
            return total + jnp.sum(value, axis=0, keepdims=True)

        total = lax.fori_loop(0, 4, second, jnp.zeros((1, 2 * SLOTS), F32))
        scale = live / total

        def third(t, carry):
            value = (logits[t] * scale).astype(BF16).reshape(4, SHARD, 2 * SLOTS)
            for i, k in enumerate(pair):
                weights[pl.ds(4 * t, 4), :, k * SLOTS : (k + 1) * SLOTS] = value[
                    :, :, i * SLOTS : (i + 1) * SLOTS
                ]
            return carry

        lax.fori_loop(0, 4, third, 0)
        affinity = SOFTMAX_TEMP * (top + jnp.log(total))
        for i, k in enumerate(pair):
            mine = jnp.broadcast_to(affinity[:, i * SLOTS : (i + 1) * SLOTS], (8, SLOTS))
            if k:
                afftx[k] = mine
                aff_copy(k).start()
            else:
                affrx[0] = mine

    for number, pair in enumerate(PAIRS):
        score(number, pair)

    part = (part_a, part_b)
    own = (own_a, own_b)
    far_in, near_in = (far_a, far_b), (near_a, near_b)
    send, last = (send_a, send_b), (last_a, last_b)

    def product(axis, index):
        if axis == 0:
            lhs = weights[pl.ds(4 * index, 4)].reshape(4 * SHARD, POOL)
        else:
            lhs = jnp.concatenate([weights[4 * i + index] for i in range(4)], axis=0)
        rhs = rx[:, :, axis * HALF : (axis + 1) * HALF].reshape(GROUPS * SLOTS, HALF)
        return jnp.dot(lhs, rhs, preferred_element_type=F32).reshape(4, SHARD, HALF)

    def share(sub):
        return pl.ds(sub * SUB, SUB)

    def hop(axis, sub, side, near, piece):
        first, second = place[axis]
        step = 1 - 2 * side
        span = pl.ds(piece * QUARTER, QUARTER)
        source = part[axis].at[turn(first, step if near else 2), :, share(sub), span]
        target = (g, member(turn(first, step), second, axis))
        if near:
            return remote(
                source,
                near_in[axis].at[side, :, share(sub), span],
                near_send.at[axis, sub, side, piece],
                near_recv.at[axis, sub, side, piece],
                target,
            )
        return remote(
            source,
            far_in[axis].at[side, :, share(sub)],
            far_send.at[axis, sub, side],
            far_recv.at[axis, sub, side],
            target,
        )

    def final(axis, sub, k):
        first, second = place[axis]
        return remote(
            send[axis].at[turn(second, k), share(sub)],
            last[axis].at[k - 1, share(sub)],
            last_send.at[axis, sub, k],
            last_recv.at[axis, sub, k],
            (g, member(first, turn(second, k), axis)),
        )

    for axis in (0, 1):
        index = turn(place[axis][0], 2)
        part[axis][index] = product(axis, index).astype(BF16)
        for side in (0, 1):
            hop(axis, 0, side, False, side).start()
    for axis in (0, 1):
        for side in (0, 1):
            index = turn(place[axis][0], 1 - 2 * side)
            part[axis][index] = product(axis, index).astype(BF16)
            hop(axis, 0, side, True, 1 - side).start()
        for side in (0, 1):
            hop(axis, 1, side, False, side).start()
    for axis in (0, 1):
        own[axis][...] = product(axis, place[axis][0])

    def relay(axis, sub, side):
        index = turn(place[axis][0], 1 - 2 * side)
        hop(axis, sub, side, False, side).wait_recv()
        rows = slice(sub * SUB, (sub + 1) * SUB)
        span = slice(side * QUARTER, (side + 1) * QUARTER)
        part[axis][index, :, rows, span] = (
            part[axis][index, :, rows, span].astype(F32) + far_in[axis][side, :, rows].astype(F32)
        ).astype(BF16)
        hop(axis, sub, side, True, side).start()

    for axis in (0, 1):
        for side in (0, 1):
            relay(axis, 0, side)
    for axis in (0, 1):
        for side in (0, 1):
            hop(axis, 1, side, True, 1 - side).start()

    lanes = iota((SHARD, BLK), 1)
    diagonal = lanes == iota((SHARD, BLK), 0)

    def total1(k):
        to = turn(z, k)
        return remote(tot1.at[to], tot1rx.at[k], tot_send.at[0, k], tot_recv.at[0, k], (g, to * 4 + y))

    def total2(k):
        to = turn(y, k)
        return remote(tot2.at[to], tot2rx.at[k], tot_send.at[1, k], tot_recv.at[1, k], (g, z * 4 + to))

    def total_of(i, carry):
        for j in range(4):
            column = jnp.sum(weights[4 * i + j].astype(F32), axis=1, keepdims=True)
            row = jnp.sum(jnp.where(diagonal, column, 0.0), axis=0, keepdims=True)
            tot1[i, j] = jnp.broadcast_to(row, (8, BLK))
        return carry

    lax.fori_loop(0, 4, total_of, 0)
    for k in range(1, 4):
        total1(k).start()

    for axis in (0, 1):
        for side in (0, 1):
            relay(axis, 1, side)

    totals = tot1[z]
    for k in range(1, 4):
        total1(k).wait_recv()
        totals = totals + tot1rx[k]
    tot2[...] = totals
    for k in range(1, 4):
        total2(k).start()

    affinity = jnp.zeros((1, ROWS), F32)
    square_eye = iota((SLOTS, SLOTS), 0) == iota((SLOTS, SLOTS), 1)
    for k in range(GROUPS):
        if k:
            aff_copy(k).wait_recv()
        column = jnp.sum(jnp.where(square_eye, affrx[k, 0:1], 0.0), axis=1, keepdims=True)
        here = slot == (slot_ids + group_at(k) * SLOTS).astype(F32)
        affinity = affinity + jnp.sum(jnp.where(here, column, 0.0), axis=0, keepdims=True)
    aff_ref[...] = affinity

    for sub in range(SUBS):
        rows = slice(sub * SUB, (sub + 1) * SUB)
        for axis in (0, 1):
            total = own[axis][:, rows]
            for side in (0, 1):
                for piece in (0, 1):
                    hop(axis, sub, side, True, piece).wait_recv()
                total = total + near_in[axis][side, :, rows].astype(F32)
            own[axis][:, rows] = total
            send[axis][:, rows] = total.astype(BF16)
            for k in (2, 1, 3):
                final(axis, sub, k).start()

    totals = tot2[y]
    for k in range(1, 4):
        total2(k).wait_recv()
        totals = totals + tot2rx[k]
    column = jnp.sum(jnp.where(diagonal, totals[0:1], 0.0), axis=1, keepdims=True) + PRIOR_WEIGHT

    for sub in range(SUBS):
        rows = slice(sub * SUB, (sub + 1) * SUB)
        for axis in (0, 1):
            total = own[axis][place[axis][1], rows]
            for k in range(1, 4):
                final(axis, sub, k).wait_recv()
                total = total + last[axis][k - 1, rows].astype(F32)
            span = slice(axis * HALF, (axis + 1) * HALF)
            prior = pool[d, rows, span].astype(F32)
            new_ref[rows, span] = (total + PRIOR_WEIGHT * prior) / column[rows]

    for k in range(1, GROUPS):
        flag_copy(k).wait_send()
        row_copy(k).wait_send()
        aff_copy(k).wait_send()
    for k in range(1, 4):
        total1(k).wait_send()
        total2(k).wait_send()
        for axis in (0, 1):
            gather1(axis, k).wait_send()
            for k1 in range(4):
                gather2(axis, k1, k).wait_send()
            for sub in range(SUBS):
                final(axis, sub, k).wait_send()
    for axis in (0, 1):
        for sub in range(SUBS):
            for side in (0, 1):
                hop(axis, sub, side, False, side).wait_send()
                for piece in (0, 1):
                    hop(axis, sub, side, True, piece).wait_send()


def local(points, coarse, candidates, centroids):
    vmem = pl.BlockSpec(memory_space=pltpu.VMEM)
    anywhere = pl.BlockSpec(memory_space=pl.ANY)
    dma = pltpu.SemaphoreType.DMA
    updated, affinity = pl.pallas_call(
        kernel,
        out_shape=(
            jax.ShapeDtypeStruct((SHARD, WIDTH), F32),
            jax.ShapeDtypeStruct((1, ROWS), F32),
        ),
        in_specs=[anywhere] * 4,
        out_specs=(vmem, vmem),
        scratch_shapes=[
            pltpu.SMEM((LISTED, CLUSTERS), jnp.int32),
            pltpu.VMEM((ROWS, WIDTH), BF16),
            pltpu.VMEM((1, ROWS), jnp.int32),
            pltpu.VMEM((GROUPS, SLOTS, WIDTH), BF16),
            pltpu.VMEM((GROUPS, SLOTS, WIDTH), BF16),
            pltpu.VMEM((GROUPS, 8, SLOTS), F32),
            pltpu.VMEM((GROUPS, 8, SLOTS), F32),
            pltpu.VMEM((MEMBERS, SHARD, WIDTH), BF16),
            pltpu.VMEM((8, BLK, SLOTS), F32),
            pltpu.VMEM((4, 4 * SHARD, 2 * SLOTS), F32),
            pltpu.VMEM((MEMBERS, SHARD, GROUPS * SLOTS), BF16),
            pltpu.VMEM((GROUPS, 8, SLOTS), F32),
            pltpu.VMEM((GROUPS, 8, SLOTS), F32),
            pltpu.VMEM((4, 4, 8, BLK), F32),
            pltpu.VMEM((4, 4, 8, BLK), F32),
            pltpu.VMEM((4, 8, BLK), F32),
            pltpu.VMEM((4, 8, BLK), F32),
            pltpu.VMEM((4, 4, SHARD, HALF), BF16),
            pltpu.VMEM((4, 4, SHARD, HALF), BF16),
            pltpu.VMEM((4, SHARD, HALF), F32),
            pltpu.VMEM((4, SHARD, HALF), F32),
            pltpu.VMEM((2, 4, SHARD, QUARTER), BF16),
            pltpu.VMEM((2, 4, SHARD, QUARTER), BF16),
            pltpu.VMEM((2, 4, SHARD, HALF), BF16),
            pltpu.VMEM((2, 4, SHARD, HALF), BF16),
            pltpu.VMEM((4, SHARD, HALF), BF16),
            pltpu.VMEM((4, SHARD, HALF), BF16),
            pltpu.VMEM((3, SHARD, HALF), BF16),
            pltpu.VMEM((3, SHARD, HALF), BF16),
            dma((4,)),
            dma((GROUPS,)),
            dma((GROUPS,)),
            dma((GROUPS,)),
            dma((GROUPS,)),
            dma((GROUPS,)),
            dma((GROUPS,)),
            dma((2, 4)),
            dma((2, 4)),
            dma((2, 4)),
            dma((2, 4)),
            dma((2, 4, 4)),
            dma((2, 4, 4)),
            dma((2, SUBS, 2)),
            dma((2, SUBS, 2)),
            dma((2, SUBS, 2, 2)),
            dma((2, SUBS, 2, 2)),
            dma((2, SUBS, 4)),
            dma((2, SUBS, 4)),
        ],
        compiler_params=pltpu.CompilerParams(
            collective_id=0, has_side_effects=True, vmem_limit_bytes=56 << 20
        ),
    )(candidates.T, points, coarse.reshape(1, ROWS), centroids)
    return updated, affinity.reshape(ROWS)


def solution(mesh):
    return jax.shard_map(
        local,
        mesh=mesh,
        in_specs=(P(("grp", "dev"), None), P(("grp", "dev"), None), P(), P(("grp", "dev"), None)),
        out_specs=(P(("grp", "dev"), None), P(("grp", "dev"))),
        check_vma=False,
    )
```

```python
import jax
import jax.numpy as jnp
from jax import lax
from jax.experimental import pallas as pl
from jax.experimental.pallas import tpu as pltpu
from jax.sharding import PartitionSpec as P

MESH = pl.DeviceIdType.MESH
F32 = jnp.float32
BF16 = jnp.bfloat16

SOFTMAX_TEMP = 0.4
PRIOR_WEIGHT = 1.0
FAR = 1e30

GROUPS = 8
MEMBERS = 16
ROWS = 512
WIDTH = 1024
SHARD = 64
POOL = MEMBERS * SHARD
PER_GROUP = 4
CLUSTERS = 32
CAP = 32
LISTED = 4
BLK = 128
SLOTS = PER_GROUP * CAP
HALF = WIDTH // 2
QUARTER = WIDTH // 4
SUBS = 2
SUB = SHARD // SUBS
ORDER = (2, 6, 3, 7, 4, 5, 1)
BATCHES = ((0, 1), (2, 6), (3, 7), (4,), (5,))


def iota(shape, axis):
    return lax.broadcasted_iota(jnp.int32, shape, axis)


def kernel(
    cand_hbm,
    points_hbm,
    coarse_hbm,
    cent_hbm,
    new_ref,
    aff_ref,
    cand,
    points,
    coarse,
    tx,
    rx,
    txf,
    rxf,
    pool,
    norms,
    logits,
    weights,
    afftx,
    affrx,
    tot1,
    tot1rx,
    tot2,
    tot2rx,
    part_a,
    part_b,
    own_a,
    own_b,
    far_a,
    far_b,
    near_a,
    near_b,
    send_a,
    send_b,
    last_a,
    last_b,
    in_sem,
    row_send,
    row_recv,
    flag_send,
    flag_recv,
    aff_send,
    aff_recv,
    tot_send,
    tot_recv,
    ag1_send,
    ag1_recv,
    ag2_send,
    ag2_recv,
    far_send,
    far_recv,
    near_send,
    near_recv,
    last_send,
    last_recv,
):
    g = lax.axis_index("grp")
    d = lax.axis_index("dev")
    x, c = lax.div(g, 2), lax.rem(g, 2)
    z, y = lax.div(d, 4), lax.rem(d, 4)

    def group_at(k):
        return lax.rem(x + k // 2, 4) * 2 + lax.rem(c + k % 2, 2)

    def group_from(k):
        return lax.rem(x + 4 - k // 2, 4) * 2 + lax.rem(c + k % 2, 2)

    def turn(value, by):
        return lax.rem(value + by + 4, 4)

    def member(first, second, axis):
        return first * 4 + second if axis == 0 else second * 4 + first

    place = ((z, y), (y, z))

    def remote(src, dst, send_sem, recv_sem, device):
        return pltpu.make_async_remote_copy(
            src_ref=src,
            dst_ref=dst,
            send_sem=send_sem,
            recv_sem=recv_sem,
            device_id=device,
            device_id_type=MESH,
        )

    barrier = pltpu.get_barrier_semaphore()
    for k in range(1, GROUPS):
        pl.semaphore_signal(barrier, inc=1, device_id=(group_at(k), d), device_id_type=MESH)
    for axis in (0, 1):
        first, second = place[axis]
        for k in range(1, 4):
            pl.semaphore_signal(
                barrier,
                inc=1,
                device_id=(g, member(turn(first, k), second, axis)),
                device_id_type=MESH,
            )

    coarse_in = pltpu.make_async_copy(coarse_hbm, coarse, in_sem.at[0])
    points_in = pltpu.make_async_copy(points_hbm, points, in_sem.at[1])
    cent_in = pltpu.make_async_copy(cent_hbm, pool.at[d], in_sem.at[2])
    cand_in = pltpu.make_async_copy(cand_hbm, cand, in_sem.at[3])
    coarse_in.start()
    points_in.start()
    cent_in.start()
    cand_in.start()

    cluster_ids = iota((CLUSTERS, ROWS), 0)
    before = (iota((ROWS, ROWS), 0) < iota((ROWS, ROWS), 1)).astype(F32).astype(BF16)
    coarse_in.wait()
    named = (coarse[...] == cluster_ids).astype(F32)
    rank = jnp.dot(named.astype(BF16), before, preferred_element_type=F32)
    slot = jnp.sum(named * (rank + (cluster_ids * CAP).astype(F32)), axis=0, keepdims=True)
    count = jnp.sum(named, axis=1, keepdims=True)
    slot_ids = iota((SLOTS, ROWS), 0)
    lane = iota((CLUSTERS, SLOTS), 1)
    lane_cluster, lane_rank = lax.div(lane, CAP), lax.rem(lane, CAP)

    def pack(k, owner, rows_ref, flag_ref):
        here = slot == (slot_ids + owner * SLOTS).astype(F32)
        rows_ref[k] = jnp.dot(
            here.astype(F32).astype(BF16), points[...], preferred_element_type=F32
        ).astype(BF16)
        mine = iota((CLUSTERS, SLOTS), 0) == lane_cluster + owner * PER_GROUP
        held = jnp.sum(jnp.where(mine, count, 0.0), axis=0, keepdims=True)
        live = (lane_rank[0:1].astype(F32) < held).astype(F32)
        flag_ref[k] = jnp.broadcast_to(live, (8, SLOTS))

    def row_copy(k):
        return remote(tx.at[k], rx.at[k], row_send.at[k], row_recv.at[k], (group_at(k), d))

    def flag_copy(k):
        return remote(txf.at[k], rxf.at[k], flag_send.at[k], flag_recv.at[k], (group_at(k), d))

    def aff_copy(k):
        return remote(afftx.at[k], affrx.at[k], aff_send.at[k], aff_recv.at[k], (group_from(k), d))

    def columns(axis):
        return pl.ds(axis * HALF, HALF)

    def gather1(axis, k):
        first, second = place[axis]
        piece = pool.at[d, :, columns(axis)]
        return remote(
            piece,
            piece,
            ag1_send.at[axis, k],
            ag1_recv.at[axis, k],
            (g, member(turn(first, k), second, axis)),
        )

    def gather2(axis, k1, k2):
        first, second = place[axis]
        piece = pool.at[member(turn(first, -k1), second, axis), :, columns(axis)]
        return remote(
            piece,
            piece,
            ag2_send.at[axis, k1, k2],
            ag2_recv.at[axis, k1, k2],
            (g, member(first, turn(second, k2), axis)),
        )

    points_in.wait()
    for k in ORDER[:2]:
        pack(k, group_at(k), tx, txf)
    cent_in.wait()
    pl.semaphore_wait(barrier, GROUPS - 1 + 6)
    for axis in (0, 1):
        for k in (2, 1, 3):
            gather1(axis, k).start()
    for i, k in enumerate(ORDER):
        if i >= 2:
            pack(k, group_at(k), tx, txf)
        row_copy(k).start()
        flag_copy(k).start()
        if i == 1:
            for axis in (0, 1):
                for k2 in (2, 1, 3):
                    gather2(axis, 0, k2).start()
    pack(0, g, rx, rxf)

    for k1 in (1, 3, 2):
        for axis in (0, 1):
            gather1(axis, k1).wait_recv()
            for k2 in (2, 1, 3):
                gather2(axis, k1, k2).start()

    cand_in.wait()
    block = iota((8, SLOTS), 0)
    allowed = jnp.zeros((8, SLOTS), jnp.bool_)
    wide_cluster = lax.div(iota((8, SLOTS), 1), CAP)
    for cluster in range(PER_GROUP):
        for j in range(LISTED):
            listed = cand[j, g * PER_GROUP + cluster]
            allowed = allowed | ((block == listed) & (wide_cluster == cluster))
    penalty = jnp.where(allowed, 0.0, FAR)

    for axis in (0, 1):
        for k1 in range(4):
            for k2 in range(1, 4):
                gather2(axis, k1, k2).wait_recv()

    for b in range(8):
        rows = pool[2 * b : 2 * b + 2].reshape(BLK, WIDTH).astype(F32)
        square = jnp.sum(rows * rows, axis=1, keepdims=True)
        norms[b] = square + penalty[b : b + 1]

    def score(number, pair):
        for k in pair:
            if k:
                row_copy(k).wait_recv()
                flag_copy(k).wait_recv()
        rows = jnp.concatenate([rx[k] for k in pair], axis=0)
        live = jnp.concatenate([rxf[k, 0:1] for k in pair], axis=1)

        wide = len(pair) * SLOTS
        top = jnp.full((1, wide), -jnp.inf, F32)
        for t in range(4):
            tile = pool[4 * t : 4 * t + 4].reshape(4 * SHARD, WIDTH)
            inner = lax.dot_general(
                tile, rows, (((1,), (1,)), ((), ())), preferred_element_type=F32
            )
            square = norms[2 * t : 2 * t + 2].reshape(4 * SHARD, SLOTS)
            square = jnp.concatenate([square] * len(pair), axis=1)
            value = (2.0 * inner - square) * (1.0 / SOFTMAX_TEMP)
            logits[t, :, :wide] = value
            top = jnp.maximum(top, jnp.max(value, axis=0, keepdims=True))
        total = jnp.zeros((1, wide), F32)
        for t in range(4):
            value = jnp.exp(logits[t, :, :wide] - top)
            logits[t, :, :wide] = value
            total = total + jnp.sum(value, axis=0, keepdims=True)
        scale = live / total
        for t in range(4):
            value = (logits[t, :, :wide] * scale).astype(BF16).reshape(4, SHARD, wide)
            for i, k in enumerate(pair):
                weights[4 * t : 4 * t + 4, :, k * SLOTS : (k + 1) * SLOTS] = value[
                    :, :, i * SLOTS : (i + 1) * SLOTS
                ]
        affinity = SOFTMAX_TEMP * (top + jnp.log(total))
        for i, k in enumerate(pair):
            mine = jnp.broadcast_to(affinity[:, i * SLOTS : (i + 1) * SLOTS], (8, SLOTS))
            if k:
                afftx[k] = mine
                aff_copy(k).start()
            else:
                affrx[0] = mine

    for number, pair in enumerate(BATCHES):
        score(number, pair)

    part = (part_a, part_b)
    own = (own_a, own_b)
    far_in, near_in = (far_a, far_b), (near_a, near_b)
    send, last = (send_a, send_b), (last_a, last_b)

    def product(axis, index):
        if axis == 0:
            lhs = weights[pl.ds(4 * index, 4)].reshape(4 * SHARD, POOL)
        else:
            lhs = jnp.concatenate([weights[4 * i + index] for i in range(4)], axis=0)
        rhs = rx[:, :, axis * HALF : (axis + 1) * HALF].reshape(GROUPS * SLOTS, HALF)
        return jnp.dot(lhs, rhs, preferred_element_type=F32).reshape(4, SHARD, HALF)

    def share(sub):
        return pl.ds(sub * SUB, SUB)

    def hop(axis, sub, side, near, piece):
        first, second = place[axis]
        step = 1 - 2 * side
        span = pl.ds(piece * QUARTER, QUARTER)
        source = part[axis].at[turn(first, step if near else 2), :, share(sub), span]
        target = (g, member(turn(first, step), second, axis))
        if near:
            return remote(
                source,
                near_in[axis].at[side, :, share(sub), span],
                near_send.at[axis, sub, side, piece],
                near_recv.at[axis, sub, side, piece],
                target,
            )
        return remote(
            source,
            far_in[axis].at[side, :, share(sub)],
            far_send.at[axis, sub, side],
            far_recv.at[axis, sub, side],
            target,
        )

    def final(axis, sub, k):
        first, second = place[axis]
        return remote(
            send[axis].at[turn(second, k), share(sub)],
            last[axis].at[k - 1, share(sub)],
            last_send.at[axis, sub, k],
            last_recv.at[axis, sub, k],
            (g, member(first, turn(second, k), axis)),
        )

    for axis in (0, 1):
        index = turn(place[axis][0], 2)
        part[axis][index] = product(axis, index).astype(BF16)
        for side in (0, 1):
            hop(axis, 0, side, False, side).start()
    for axis in (0, 1):
        for side in (0, 1):
            index = turn(place[axis][0], 1 - 2 * side)
            part[axis][index] = product(axis, index).astype(BF16)
            hop(axis, 0, side, True, 1 - side).start()
        for side in (0, 1):
            hop(axis, 1, side, False, side).start()
    for axis in (0, 1):
        own[axis][...] = product(axis, place[axis][0])

    def relay(axis, sub, side):
        index = turn(place[axis][0], 1 - 2 * side)
        hop(axis, sub, side, False, side).wait_recv()
        rows = slice(sub * SUB, (sub + 1) * SUB)
        span = slice(side * QUARTER, (side + 1) * QUARTER)
        part[axis][index, :, rows, span] = (
            part[axis][index, :, rows, span].astype(F32) + far_in[axis][side, :, rows].astype(F32)
        ).astype(BF16)
        hop(axis, sub, side, True, side).start()

    for axis in (0, 1):
        for side in (0, 1):
            relay(axis, 0, side)
    for axis in (0, 1):
        for side in (0, 1):
            hop(axis, 1, side, True, 1 - side).start()

    lanes = iota((SHARD, BLK), 1)
    diagonal = lanes == iota((SHARD, BLK), 0)

    def total1(k):
        to = turn(z, k)
        return remote(tot1.at[to], tot1rx.at[k], tot_send.at[0, k], tot_recv.at[0, k], (g, to * 4 + y))

    def total2(k):
        to = turn(y, k)
        return remote(tot2.at[to], tot2rx.at[k], tot_send.at[1, k], tot_recv.at[1, k], (g, z * 4 + to))

    def total_of(i, carry):
        for j in range(4):
            column = jnp.sum(weights[4 * i + j].astype(F32), axis=1, keepdims=True)
            row = jnp.sum(jnp.where(diagonal, column, 0.0), axis=0, keepdims=True)
            tot1[i, j] = jnp.broadcast_to(row, (8, BLK))
        return carry

    lax.fori_loop(0, 4, total_of, 0)
    for k in range(1, 4):
        total1(k).start()

    for axis in (0, 1):
        for side in (0, 1):
            relay(axis, 1, side)

    totals = tot1[z]
    for k in range(1, 4):
        total1(k).wait_recv()
        totals = totals + tot1rx[k]
    tot2[...] = totals
    for k in range(1, 4):
        total2(k).start()

    affinity = jnp.zeros((1, ROWS), F32)
    square_eye = iota((SLOTS, SLOTS), 0) == iota((SLOTS, SLOTS), 1)
    for k in range(GROUPS):
        if k:
            aff_copy(k).wait_recv()
        column = jnp.sum(jnp.where(square_eye, affrx[k, 0:1], 0.0), axis=1, keepdims=True)
        here = slot == (slot_ids + group_at(k) * SLOTS).astype(F32)
        affinity = affinity + jnp.sum(jnp.where(here, column, 0.0), axis=0, keepdims=True)
    aff_ref[...] = affinity.reshape(ROWS)

    for sub in range(SUBS):
        rows = slice(sub * SUB, (sub + 1) * SUB)
        for axis in (0, 1):
            total = own[axis][:, rows]
            for side in (0, 1):
                for piece in (0, 1):
                    hop(axis, sub, side, True, piece).wait_recv()
                total = total + near_in[axis][side, :, rows].astype(F32)
            own[axis][:, rows] = total
            send[axis][:, rows] = total.astype(BF16)
            for k in (2, 1, 3):
                final(axis, sub, k).start()

    totals = tot2[y]
    for k in range(1, 4):
        total2(k).wait_recv()
        totals = totals + tot2rx[k]
    column = jnp.sum(jnp.where(diagonal, totals[0:1], 0.0), axis=1, keepdims=True) + PRIOR_WEIGHT

    for sub in range(SUBS):
        rows = slice(sub * SUB, (sub + 1) * SUB)
        for axis in (0, 1):
            total = own[axis][place[axis][1], rows]
            for k in range(1, 4):
                final(axis, sub, k).wait_recv()
                total = total + last[axis][k - 1, rows].astype(F32)
            span = slice(axis * HALF, (axis + 1) * HALF)
            prior = pool[d, rows, span].astype(F32)
            new_ref[rows, span] = (total + PRIOR_WEIGHT * prior) / column[rows]

    for k in range(1, GROUPS):
        flag_copy(k).wait_send()
        row_copy(k).wait_send()
        aff_copy(k).wait_send()
    for k in range(1, 4):
        total1(k).wait_send()
        total2(k).wait_send()
        for axis in (0, 1):
            gather1(axis, k).wait_send()
            for k1 in range(4):
                gather2(axis, k1, k).wait_send()
            for sub in range(SUBS):
                final(axis, sub, k).wait_send()
    for axis in (0, 1):
        for sub in range(SUBS):
            for side in (0, 1):
                hop(axis, sub, side, False, side).wait_send()
                for piece in (0, 1):
                    hop(axis, sub, side, True, piece).wait_send()


def local(points, coarse, candidates, centroids):
    operands = (candidates.T, points, coarse.reshape(1, ROWS), centroids)
    vmem = pl.BlockSpec(memory_space=pltpu.VMEM)
    anywhere = pl.BlockSpec(memory_space=pl.ANY)
    dma = pltpu.SemaphoreType.DMA
    updated, affinity = pl.pallas_call(
        kernel,
        out_shape=(
            jax.ShapeDtypeStruct((SHARD, WIDTH), F32),
            jax.ShapeDtypeStruct((ROWS,), F32),
        ),
        in_specs=[anywhere] * 4,
        out_specs=(vmem, vmem),
        scratch_shapes=[
            pltpu.SMEM((LISTED, CLUSTERS), jnp.int32),
            pltpu.VMEM((ROWS, WIDTH), BF16),
            pltpu.VMEM((1, ROWS), jnp.int32),
            pltpu.VMEM((GROUPS, SLOTS, WIDTH), BF16),
            pltpu.VMEM((GROUPS, SLOTS, WIDTH), BF16),
            pltpu.VMEM((GROUPS, 8, SLOTS), F32),
            pltpu.VMEM((GROUPS, 8, SLOTS), F32),
            pltpu.VMEM((MEMBERS, SHARD, WIDTH), BF16),
            pltpu.VMEM((8, BLK, SLOTS), F32),
            pltpu.VMEM((4, 4 * SHARD, 2 * SLOTS), F32),
            pltpu.VMEM((MEMBERS, SHARD, GROUPS * SLOTS), BF16),
            pltpu.VMEM((GROUPS, 8, SLOTS), F32),
            pltpu.VMEM((GROUPS, 8, SLOTS), F32),
            pltpu.VMEM((4, 4, 8, BLK), F32),
            pltpu.VMEM((4, 4, 8, BLK), F32),
            pltpu.VMEM((4, 8, BLK), F32),
            pltpu.VMEM((4, 8, BLK), F32),
            pltpu.VMEM((4, 4, SHARD, HALF), BF16),
            pltpu.VMEM((4, 4, SHARD, HALF), BF16),
            pltpu.VMEM((4, SHARD, HALF), F32),
            pltpu.VMEM((4, SHARD, HALF), F32),
            pltpu.VMEM((2, 4, SHARD, QUARTER), BF16),
            pltpu.VMEM((2, 4, SHARD, QUARTER), BF16),
            pltpu.VMEM((2, 4, SHARD, HALF), BF16),
            pltpu.VMEM((2, 4, SHARD, HALF), BF16),
            pltpu.VMEM((4, SHARD, HALF), BF16),
            pltpu.VMEM((4, SHARD, HALF), BF16),
            pltpu.VMEM((3, SHARD, HALF), BF16),
            pltpu.VMEM((3, SHARD, HALF), BF16),
            dma((4,)),
            dma((GROUPS,)),
            dma((GROUPS,)),
            dma((GROUPS,)),
            dma((GROUPS,)),
            dma((GROUPS,)),
            dma((GROUPS,)),
            dma((2, 4)),
            dma((2, 4)),
            dma((2, 4)),
            dma((2, 4)),
            dma((2, 4, 4)),
            dma((2, 4, 4)),
            dma((2, SUBS, 2)),
            dma((2, SUBS, 2)),
            dma((2, SUBS, 2, 2)),
            dma((2, SUBS, 2, 2)),
            dma((2, SUBS, 4)),
            dma((2, SUBS, 4)),
        ],
        compiler_params=pltpu.CompilerParams(
            collective_id=0, has_side_effects=True, vmem_limit_bytes=32 << 20
        ),
    )(*(pltpu.with_memory_space_constraint(a, pltpu.HBM) for a in operands))
    return updated, affinity


def solution(mesh):
    return jax.shard_map(
        local,
        mesh=mesh,
        in_specs=(P(("grp", "dev"), None), P(("grp", "dev"), None), P(), P(("grp", "dev"), None)),
        out_specs=(P(("grp", "dev"), None), P(("grp", "dev"))),
        check_vma=False,
    )
```

```python
import jax
import jax.numpy as jnp
from jax import lax
from jax.experimental import pallas as pl
from jax.experimental.pallas import tpu as pltpu
from jax.sharding import PartitionSpec as P

MESH = pl.DeviceIdType.MESH
F32 = jnp.float32
BF16 = jnp.bfloat16

SOFTMAX_TEMP = 0.4
PRIOR_WEIGHT = 1.0
FAR = 1e30

GROUPS = 8
MEMBERS = 16
ROWS = 512
WIDTH = 1024
SHARD = 64
POOL = MEMBERS * SHARD
PER_GROUP = 4
CLUSTERS = 32
CAP = 32
LISTED = 4
BLK = 128
SLOTS = PER_GROUP * CAP
HALF = WIDTH // 2
QUARTER = WIDTH // 4
SUBS = 2
SUB = SHARD // SUBS
AWAY = ((0, 0), (0, 1), (1, 0), (3, 0), (1, 1), (3, 1), (2, 0), (2, 1))
ORDER = (2, 3, 4, 5, 6, 7, 1)
BATCHES = ((0, 1), (2, 3), (4, 5), (6,), (7,))


def iota(shape, axis):
    return lax.broadcasted_iota(jnp.int32, shape, axis)


def kernel(
    cand_hbm,
    points_hbm,
    coarse_hbm,
    cent_hbm,
    new_ref,
    aff_ref,
    cand,
    points,
    coarse,
    tx,
    rx,
    txf,
    rxf,
    pool,
    norms,
    logits,
    weights,
    afftx,
    affrx,
    tot1,
    tot1rx,
    tot2,
    tot2rx,
    part_a,
    part_b,
    own_a,
    own_b,
    far_a,
    far_b,
    near_a,
    near_b,
    send_a,
    send_b,
    last_a,
    last_b,
    in_sem,
    row_send,
    row_recv,
    flag_sem,
    aff_sem,
    tot_sem,
    ag_send,
    ag1_recv,
    ag2_recv,
    part_send,
    far_recv,
    near_recv,
    last_send,
    last_recv,
):
    g = lax.axis_index("grp")
    d = lax.axis_index("dev")
    x, c = lax.div(g, 2), lax.rem(g, 2)
    z, y = lax.div(d, 4), lax.rem(d, 4)

    def group_at(k):
        return lax.rem(x + AWAY[k][0], 4) * 2 + lax.rem(c + AWAY[k][1], 2)

    def group_from(k):
        return lax.rem(x + 4 - AWAY[k][0], 4) * 2 + lax.rem(c + AWAY[k][1], 2)

    def turn(value, by):
        return lax.rem(value + by + 4, 4)

    def member(first, second, axis):
        return first * 4 + second if axis == 0 else second * 4 + first

    place = ((z, y), (y, z))

    def remote(src, dst, send_sem, recv_sem, device):
        return pltpu.make_async_remote_copy(
            src_ref=src,
            dst_ref=dst,
            send_sem=send_sem,
            recv_sem=recv_sem,
            device_id=device,
            device_id_type=MESH,
        )

    barrier = pltpu.get_barrier_semaphore()
    for k in range(1, GROUPS):
        pl.semaphore_signal(barrier, inc=1, device_id=(group_at(k), d), device_id_type=MESH)
    for axis in (0, 1):
        first, second = place[axis]
        for k in range(1, 4):
            pl.semaphore_signal(
                barrier,
                inc=1,
                device_id=(g, member(turn(first, k), second, axis)),
                device_id_type=MESH,
            )

    coarse_in = pltpu.make_async_copy(coarse_hbm, coarse, in_sem.at[0])
    points_in = pltpu.make_async_copy(points_hbm, points, in_sem.at[1])
    cent_in = pltpu.make_async_copy(cent_hbm, pool.at[d], in_sem.at[2])
    cand_in = pltpu.make_async_copy(cand_hbm, cand, in_sem.at[3])
    coarse_in.start()
    points_in.start()
    cent_in.start()
    cand_in.start()

    cluster_ids = iota((CLUSTERS, ROWS), 0)
    before = (iota((ROWS, ROWS), 0) < iota((ROWS, ROWS), 1)).astype(F32).astype(BF16)
    coarse_in.wait()
    named = (coarse[...] == cluster_ids).astype(F32)
    rank = jnp.dot(named.astype(BF16), before, preferred_element_type=F32)
    slot = jnp.sum(named * (rank + (cluster_ids * CAP).astype(F32)), axis=0, keepdims=True)
    count = jnp.sum(named, axis=1, keepdims=True)
    slot_ids = iota((SLOTS, ROWS), 0)
    lane = iota((CLUSTERS, SLOTS), 1)
    lane_cluster, lane_rank = lax.div(lane, CAP), lax.rem(lane, CAP)

    def flag(owner):
        mine = iota((CLUSTERS, SLOTS), 0) == lane_cluster + owner * PER_GROUP
        held = jnp.sum(jnp.where(mine, count, 0.0), axis=0, keepdims=True)
        live = (lane_rank[0:1].astype(F32) < held).astype(F32)
        return jnp.broadcast_to(live, (8, SLOTS))

    def pack(owner):
        here = slot == (slot_ids + owner * SLOTS).astype(F32)
        return jnp.dot(
            here.astype(F32).astype(BF16), points[...], preferred_element_type=F32
        ).astype(BF16)

    def row_copy(k):
        number = [k in batch for batch in BATCHES].index(True)
        return remote(tx.at[k], rx.at[k], row_send, row_recv.at[number], (group_at(k), d))

    def flag_copy(k):
        return remote(txf.at[k], rxf.at[k], flag_sem.at[0], flag_sem.at[1], (group_at(k), d))

    def aff_copy(k):
        return remote(afftx.at[k], affrx.at[k], aff_sem.at[0], aff_sem.at[1], (group_from(k), d))

    def arrived(ref, sem):
        remote(ref, ref, sem, sem, (g, d)).wait_recv()

    def left(ref, sem):
        remote(ref, ref, sem, sem, (g, d)).wait_send()

    def columns(axis):
        return pl.ds(axis * HALF, HALF)

    def gather1(axis, k):
        first, second = place[axis]
        piece = pool.at[d, :, columns(axis)]
        return remote(
            piece,
            piece,
            ag_send,
            ag1_recv.at[axis, k - 1],
            (g, member(turn(first, k), second, axis)),
        )

    def gather2(axis, k1, k2):
        first, second = place[axis]
        piece = pool.at[member(turn(first, -k1), second, axis), :, columns(axis)]
        return remote(
            piece,
            piece,
            ag_send,
            ag2_recv,
            (g, member(first, turn(second, k2), axis)),
        )

    for k in ORDER:
        txf[k] = flag(group_at(k))
    rxf[0] = flag(g)
    points_in.wait()
    for k in ORDER[:2]:
        tx[k] = pack(group_at(k))
    cent_in.wait()
    pl.semaphore_wait(barrier, GROUPS - 1 + 6)
    for axis in (0, 1):
        for k in (2, 1, 3):
            gather1(axis, k).start()
    for k in ORDER:
        flag_copy(k).start()
    for i, k in enumerate(ORDER):
        if i >= 2:
            tx[k] = pack(group_at(k))
        row_copy(k).start()
        if i == 1:
            for axis in (0, 1):
                for k2 in (2, 1, 3):
                    gather2(axis, 0, k2).start()
    rx[0] = pack(g)

    for k1 in (1, 3, 2):
        for axis in (0, 1):
            gather1(axis, k1).wait_recv()
            for k2 in (2, 1, 3):
                gather2(axis, k1, k2).start()

    cand_in.wait()
    block = iota((8, SLOTS), 0)
    allowed = jnp.zeros((8, SLOTS), jnp.bool_)
    wide_cluster = lax.div(iota((8, SLOTS), 1), CAP)
    for cluster in range(PER_GROUP):
        for j in range(LISTED):
            listed = cand[j, g * PER_GROUP + cluster]
            allowed = allowed | ((block == listed) & (wide_cluster == cluster))
    penalty = jnp.where(allowed, 0.0, FAR)

    arrived(pool.at[0:12], ag2_recv)
    arrived(rxf.at[1:GROUPS], flag_sem.at[1])

    for b in range(8):
        rows = pool[2 * b : 2 * b + 2].reshape(BLK, WIDTH).astype(F32)
        square = jnp.sum(rows * rows, axis=1, keepdims=True)
        norms[b] = square + penalty[b : b + 1]

    def score(number, pair):
        first = max(pair[0], 1)
        arrived(rx.at[first : pair[-1] + 1], row_recv.at[number])
        rows = rx[pair[0] : pair[-1] + 1].reshape(len(pair) * SLOTS, WIDTH)
        live = jnp.concatenate([rxf[k, 0:1] for k in pair], axis=1)

        wide = len(pair) * SLOTS
        top = jnp.full((1, wide), -jnp.inf, F32)
        for t in range(4):
            tile = pool[4 * t : 4 * t + 4].reshape(4 * SHARD, WIDTH)
            inner = lax.dot_general(
                tile, rows, (((1,), (1,)), ((), ())), preferred_element_type=F32
            )
            square = norms[2 * t : 2 * t + 2].reshape(4 * SHARD, SLOTS)
            square = jnp.concatenate([square] * len(pair), axis=1)
            value = (2.0 * inner - square) * (1.0 / SOFTMAX_TEMP)
            logits[t, :, :wide] = value
            top = jnp.maximum(top, jnp.max(value, axis=0, keepdims=True))
        total = jnp.zeros((1, wide), F32)
        for t in range(4):
            value = jnp.exp(logits[t, :, :wide] - top)
            logits[t, :, :wide] = value
            total = total + jnp.sum(value, axis=0, keepdims=True)
        scale = live / total
        for t in range(4):
            value = (logits[t, :, :wide] * scale).astype(BF16).reshape(4, SHARD, wide)
            weights[4 * t : 4 * t + 4, :, pair[0] * SLOTS : (pair[-1] + 1) * SLOTS] = value
        affinity = SOFTMAX_TEMP * (top + jnp.log(total))
        for i, k in enumerate(pair):
            mine = jnp.broadcast_to(affinity[:, i * SLOTS : (i + 1) * SLOTS], (8, SLOTS))
            if k:
                afftx[k] = mine
                aff_copy(k).start()
            else:
                affrx[0] = mine

    for number, pair in enumerate(BATCHES):
        score(number, pair)

    part = (part_a, part_b)
    own = (own_a, own_b)
    far_in, near_in = (far_a, far_b), (near_a, near_b)
    send, last = (send_a, send_b), (last_a, last_b)

    def product(axis, index):
        if axis == 0:
            lhs = weights[pl.ds(4 * index, 4)].reshape(4 * SHARD, POOL)
        else:
            lhs = jnp.concatenate([weights[4 * i + index] for i in range(4)], axis=0)
        rhs = rx[:, :, axis * HALF : (axis + 1) * HALF].reshape(GROUPS * SLOTS, HALF)
        return jnp.dot(lhs, rhs, preferred_element_type=F32).reshape(4, SHARD, HALF)

    def share(sub):
        return pl.ds(sub * SUB, SUB)

    def hop(axis, sub, side, near, piece):
        first, second = place[axis]
        step = 1 - 2 * side
        span = pl.ds(piece * QUARTER, QUARTER)
        source = part[axis].at[turn(first, step if near else 2), :, share(sub), span]
        target = (g, member(turn(first, step), second, axis))
        if near:
            return remote(
                source,
                near_in[axis].at[side, :, share(sub), span],
                part_send.at[axis],
                near_recv.at[axis, sub],
                target,
            )
        return remote(
            source,
            far_in[axis].at[side, :, share(sub)],
            part_send.at[axis],
            far_recv.at[axis, sub],
            target,
        )

    def final(axis, sub, k):
        first, second = place[axis]
        return remote(
            send[axis].at[turn(second, k), share(sub)],
            last[axis].at[k - 1, share(sub)],
            last_send.at[axis],
            last_recv.at[axis, sub],
            (g, member(first, turn(second, k), axis)),
        )

    for axis in (0, 1):
        index = turn(place[axis][0], 2)
        part[axis][index] = product(axis, index).astype(BF16)
        for side in (0, 1):
            hop(axis, 0, side, False, side).start()
    for axis in (0, 1):
        for side in (0, 1):
            index = turn(place[axis][0], 1 - 2 * side)
            part[axis][index] = product(axis, index).astype(BF16)
            hop(axis, 0, side, True, 1 - side).start()
        for side in (0, 1):
            hop(axis, 1, side, False, side).start()
    for axis in (0, 1):
        own[axis][...] = product(axis, place[axis][0])

    def relay(axis, sub):
        rows = slice(sub * SUB, (sub + 1) * SUB)
        arrived(far_in[axis].at[:, :, share(sub)], far_recv.at[axis, sub])
        for side in (0, 1):
            index = turn(place[axis][0], 1 - 2 * side)
            span = slice(side * QUARTER, (side + 1) * QUARTER)
            part[axis][index, :, rows, span] = (
                part[axis][index, :, rows, span].astype(F32)
                + far_in[axis][side, :, rows].astype(F32)
            ).astype(BF16)
            hop(axis, sub, side, True, side).start()

    for axis in (0, 1):
        relay(axis, 0)
    for axis in (0, 1):
        for side in (0, 1):
            hop(axis, 1, side, True, 1 - side).start()

    lanes = iota((SHARD, BLK), 1)
    diagonal = lanes == iota((SHARD, BLK), 0)

    def total1(k):
        to = turn(z, k)
        return remote(tot1.at[to], tot1rx.at[k], tot_sem.at[0], tot_sem.at[1], (g, to * 4 + y))

    def total2(k):
        to = turn(y, k)
        return remote(tot2.at[to], tot2rx.at[k], tot_sem.at[2], tot_sem.at[3], (g, z * 4 + to))

    def total_of(i, carry):
        for j in range(4):
            column = jnp.sum(weights[4 * i + j].astype(F32), axis=1, keepdims=True)
            row = jnp.sum(jnp.where(diagonal, column, 0.0), axis=0, keepdims=True)
            tot1[i, j] = jnp.broadcast_to(row, (8, BLK))
        return carry

    lax.fori_loop(0, 4, total_of, 0)
    for k in range(1, 4):
        total1(k).start()

    for axis in (0, 1):
        relay(axis, 1)

    arrived(tot1rx.at[1:4], tot_sem.at[1])
    totals = tot1[z]
    for k in range(1, 4):
        totals = totals + tot1rx[k]
    tot2[...] = totals
    for k in range(1, 4):
        total2(k).start()

    affinity = jnp.zeros((1, ROWS), F32)
    square_eye = iota((SLOTS, SLOTS), 0) == iota((SLOTS, SLOTS), 1)
    arrived(affrx.at[1:GROUPS], aff_sem.at[1])
    for k in range(GROUPS):
        column = jnp.sum(jnp.where(square_eye, affrx[k, 0:1], 0.0), axis=1, keepdims=True)
        here = slot == (slot_ids + group_at(k) * SLOTS).astype(F32)
        affinity = affinity + jnp.sum(jnp.where(here, column, 0.0), axis=0, keepdims=True)
    aff_ref[...] = affinity.reshape(ROWS)

    for sub in range(SUBS):
        rows = slice(sub * SUB, (sub + 1) * SUB)
        for axis in (0, 1):
            total = own[axis][:, rows]
            arrived(near_in[axis].at[:, :, share(sub)], near_recv.at[axis, sub])
            for side in (0, 1):
                total = total + near_in[axis][side, :, rows].astype(F32)
            own[axis][:, rows] = total
            send[axis][:, rows] = total.astype(BF16)
            for k in (2, 1, 3):
                final(axis, sub, k).start()

    totals = tot2[y]
    arrived(tot2rx.at[1:4], tot_sem.at[3])
    for k in range(1, 4):
        totals = totals + tot2rx[k]
    column = jnp.sum(jnp.where(diagonal, totals[0:1], 0.0), axis=1, keepdims=True) + PRIOR_WEIGHT

    for sub in range(SUBS):
        rows = slice(sub * SUB, (sub + 1) * SUB)
        for axis in (0, 1):
            total = own[axis][place[axis][1], rows]
            arrived(last[axis].at[:, share(sub)], last_recv.at[axis, sub])
            for k in range(1, 4):
                total = total + last[axis][k - 1, rows].astype(F32)
            span = slice(axis * HALF, (axis + 1) * HALF)
            prior = pool[d, rows, span].astype(F32)
            new_ref[rows, span] = (total + PRIOR_WEIGHT * prior) / column[rows]

    left(tx.at[1:GROUPS], row_send)
    left(txf.at[1:GROUPS], flag_sem.at[0])
    left(afftx.at[1:GROUPS], aff_sem.at[0])
    left(tot1.at[0:3], tot_sem.at[0])
    left(tot2.at[0:3], tot_sem.at[2])
    left(pool.at[0:15], ag_send)
    for axis in (0, 1):
        left(part[axis].at[0:3], part_send.at[axis])
        left(last[axis], last_send.at[axis])


def local(points, coarse, candidates, centroids):
    operands = (candidates.T, points, coarse.reshape(1, ROWS), centroids)
    vmem = pl.BlockSpec(memory_space=pltpu.VMEM)
    anywhere = pl.BlockSpec(memory_space=pl.ANY)
    dma = pltpu.SemaphoreType.DMA
    updated, affinity = pl.pallas_call(
        kernel,
        out_shape=(
            jax.ShapeDtypeStruct((SHARD, WIDTH), F32),
            jax.ShapeDtypeStruct((ROWS,), F32),
        ),
        in_specs=[anywhere] * 4,
        out_specs=(vmem, vmem),
        scratch_shapes=[
            pltpu.SMEM((LISTED, CLUSTERS), jnp.int32),
            pltpu.VMEM((ROWS, WIDTH), BF16),
            pltpu.VMEM((1, ROWS), jnp.int32),
            pltpu.VMEM((GROUPS, SLOTS, WIDTH), BF16),
            pltpu.VMEM((GROUPS, SLOTS, WIDTH), BF16),
            pltpu.VMEM((GROUPS, 8, SLOTS), F32),
            pltpu.VMEM((GROUPS, 8, SLOTS), F32),
            pltpu.VMEM((MEMBERS, SHARD, WIDTH), BF16),
            pltpu.VMEM((8, BLK, SLOTS), F32),
            pltpu.VMEM((4, 4 * SHARD, 2 * SLOTS), F32),
            pltpu.VMEM((MEMBERS, SHARD, GROUPS * SLOTS), BF16),
            pltpu.VMEM((GROUPS, 8, SLOTS), F32),
            pltpu.VMEM((GROUPS, 8, SLOTS), F32),
            pltpu.VMEM((4, 4, 8, BLK), F32),
            pltpu.VMEM((4, 4, 8, BLK), F32),
            pltpu.VMEM((4, 8, BLK), F32),
            pltpu.VMEM((4, 8, BLK), F32),
            pltpu.VMEM((4, 4, SHARD, HALF), BF16),
            pltpu.VMEM((4, 4, SHARD, HALF), BF16),
            pltpu.VMEM((4, SHARD, HALF), F32),
            pltpu.VMEM((4, SHARD, HALF), F32),
            pltpu.VMEM((2, 4, SHARD, QUARTER), BF16),
            pltpu.VMEM((2, 4, SHARD, QUARTER), BF16),
            pltpu.VMEM((2, 4, SHARD, HALF), BF16),
            pltpu.VMEM((2, 4, SHARD, HALF), BF16),
            pltpu.VMEM((4, SHARD, HALF), BF16),
            pltpu.VMEM((4, SHARD, HALF), BF16),
            pltpu.VMEM((3, SHARD, HALF), BF16),
            pltpu.VMEM((3, SHARD, HALF), BF16),
            dma((4,)),
            dma,
            dma((len(BATCHES),)),
            dma((2,)),
            dma((2,)),
            dma((4,)),
            dma,
            dma((2, 3)),
            dma,
            dma((2,)),
            dma((2, SUBS)),
            dma((2, SUBS)),
            dma((2,)),
            dma((2, SUBS)),
        ],
        compiler_params=pltpu.CompilerParams(
            collective_id=0, has_side_effects=True, vmem_limit_bytes=32 << 20
        ),
    )(*(pltpu.with_memory_space_constraint(a, pltpu.HBM) for a in operands))
    return updated, affinity


def solution(mesh):
    return jax.shard_map(
        local,
        mesh=mesh,
        in_specs=(P(("grp", "dev"), None), P(("grp", "dev"), None), P(), P(("grp", "dev"), None)),
        out_specs=(P(("grp", "dev"), None), P(("grp", "dev"))),
        check_vma=False,
    )
```

```python
import jax
import jax.numpy as jnp
from jax import lax
from jax.experimental import pallas as pl
from jax.experimental.pallas import tpu as pltpu
from jax.sharding import PartitionSpec as P

MESH = pl.DeviceIdType.MESH
F32 = jnp.float32
BF16 = jnp.bfloat16

SOFTMAX_TEMP = 0.4
PRIOR_WEIGHT = 1.0
FAR = 1e30

GROUPS = 8
MEMBERS = 16
ROWS = 512
WIDTH = 1024
SHARD = 64
POOL = MEMBERS * SHARD
PER_GROUP = 4
CLUSTERS = 32
CAP = 32
LISTED = 4
BLK = 128
SLOTS = PER_GROUP * CAP
HALF = WIDTH // 2
QUARTER = WIDTH // 4
SPANS = ((0, 1), (1, 2), (2, 4))
SUBS = len(SPANS)
AWAY = ((0, 0), (0, 1), (1, 0), (3, 0), (1, 1), (3, 1), (2, 0), (2, 1))
ORDER = (2, 3, 4, 5, 6, 7, 1)
BATCHES = ((0, 1), (2, 3), (4, 5), (6,), (7,))


def iota(shape, axis):
    return lax.broadcasted_iota(jnp.int32, shape, axis)


def kernel(
    cand_hbm,
    points_hbm,
    coarse_hbm,
    cent_hbm,
    new_ref,
    aff_ref,
    cand,
    points,
    coarse,
    tx,
    rx,
    txf,
    rxf,
    pool,
    norms,
    logits,
    weights,
    afftx,
    affrx,
    tot1,
    tot1rx,
    tot2,
    tot2rx,
    part_a,
    part_b,
    own_a,
    own_b,
    far_a,
    far_b,
    near_a,
    near_b,
    send_a,
    send_b,
    last_a,
    last_b,
    in_sem,
    row_send,
    row_recv,
    flag_sem,
    aff_sem,
    tot_sem,
    ag_send,
    ag1_recv,
    ag2_recv,
    part_send,
    far_recv,
    near_recv,
    last_send,
    last_recv,
):
    g = lax.axis_index("grp")
    d = lax.axis_index("dev")
    x, c = lax.div(g, 2), lax.rem(g, 2)
    z, y = lax.div(d, 4), lax.rem(d, 4)

    def group_at(k):
        return lax.rem(x + AWAY[k][0], 4) * 2 + lax.rem(c + AWAY[k][1], 2)

    def group_from(k):
        return lax.rem(x + 4 - AWAY[k][0], 4) * 2 + lax.rem(c + AWAY[k][1], 2)

    def turn(value, by):
        return lax.rem(value + by + 4, 4)

    def member(first, second, axis):
        return first * 4 + second if axis == 0 else second * 4 + first

    place = ((z, y), (y, z))

    def remote(src, dst, send_sem, recv_sem, device):
        return pltpu.make_async_remote_copy(
            src_ref=src,
            dst_ref=dst,
            send_sem=send_sem,
            recv_sem=recv_sem,
            device_id=device,
            device_id_type=MESH,
        )

    barrier = pltpu.get_barrier_semaphore()
    for k in range(1, GROUPS):
        pl.semaphore_signal(barrier, inc=1, device_id=(group_at(k), d), device_id_type=MESH)
    for axis in (0, 1):
        first, second = place[axis]
        for k in range(1, 4):
            pl.semaphore_signal(
                barrier,
                inc=1,
                device_id=(g, member(turn(first, k), second, axis)),
                device_id_type=MESH,
            )

    coarse_in = pltpu.make_async_copy(coarse_hbm, coarse, in_sem.at[0])
    points_in = pltpu.make_async_copy(points_hbm, points, in_sem.at[1])
    cent_in = pltpu.make_async_copy(cent_hbm, pool.at[d], in_sem.at[2])
    cand_in = pltpu.make_async_copy(cand_hbm, cand, in_sem.at[3])
    coarse_in.start()
    points_in.start()
    cent_in.start()
    cand_in.start()

    cluster_ids = iota((CLUSTERS, ROWS), 0)
    before = (iota((ROWS, ROWS), 0) < iota((ROWS, ROWS), 1)).astype(F32).astype(BF16)
    coarse_in.wait()
    named = (coarse[...] == cluster_ids).astype(F32)
    rank = jnp.dot(named.astype(BF16), before, preferred_element_type=F32)
    slot = jnp.sum(named * (rank + (cluster_ids * CAP).astype(F32)), axis=0, keepdims=True)
    count = jnp.sum(named, axis=1, keepdims=True)
    slot_ids = iota((SLOTS, ROWS), 0)
    lane = iota((CLUSTERS, SLOTS), 1)
    lane_cluster, lane_rank = lax.div(lane, CAP), lax.rem(lane, CAP)

    def flag(owner):
        mine = iota((CLUSTERS, SLOTS), 0) == lane_cluster + owner * PER_GROUP
        held = jnp.sum(jnp.where(mine, count, 0.0), axis=0, keepdims=True)
        live = (lane_rank[0:1].astype(F32) < held).astype(F32)
        return jnp.broadcast_to(live, (8, SLOTS))

    def pack(owner):
        here = slot == (slot_ids + owner * SLOTS).astype(F32)
        return jnp.dot(
            here.astype(F32).astype(BF16), points[...], preferred_element_type=F32
        ).astype(BF16)

    def row_copy(k):
        number = [k in batch for batch in BATCHES].index(True)
        return remote(tx.at[k], rx.at[k], row_send, row_recv.at[number], (group_at(k), d))

    def flag_copy(k):
        return remote(txf.at[k], rxf.at[k], flag_sem.at[0], flag_sem.at[1], (group_at(k), d))

    def aff_copy(k):
        return remote(afftx.at[k], affrx.at[k], aff_sem.at[0], aff_sem.at[1], (group_from(k), d))

    def arrived(ref, sem):
        remote(ref, ref, sem, sem, (g, d)).wait_recv()

    def left(ref, sem):
        remote(ref, ref, sem, sem, (g, d)).wait_send()

    def columns(axis):
        return pl.ds(axis * HALF, HALF)

    def gather1(axis, k):
        first, second = place[axis]
        piece = pool.at[d, :, columns(axis)]
        return remote(
            piece,
            piece,
            ag_send,
            ag1_recv.at[axis, k - 1],
            (g, member(turn(first, k), second, axis)),
        )

    def gather2(axis, k1, k2):
        first, second = place[axis]
        piece = pool.at[member(turn(first, -k1), second, axis), :, columns(axis)]
        return remote(
            piece,
            piece,
            ag_send,
            ag2_recv,
            (g, member(first, turn(second, k2), axis)),
        )

    for k in ORDER:
        txf[k] = flag(group_at(k))
    rxf[0] = flag(g)
    points_in.wait()
    tx[ORDER[0]] = pack(group_at(ORDER[0]))
    pl.semaphore_wait(barrier, GROUPS - 1 + 6)
    for i, k in enumerate(ORDER):
        if i:
            tx[k] = pack(group_at(k))
        row_copy(k).start()
        if i == 1:
            for k1 in ORDER:
                flag_copy(k1).start()
            cent_in.wait()
            for axis in (0, 1):
                for k1 in (2, 1, 3):
                    gather1(axis, k1).start()
        if i == 2:
            for axis in (0, 1):
                for k2 in (2, 1, 3):
                    gather2(axis, 0, k2).start()
    rx[0] = pack(g)

    for k1 in (1, 3, 2):
        for axis in (0, 1):
            gather1(axis, k1).wait_recv()
            for k2 in (2, 1, 3):
                gather2(axis, k1, k2).start()

    cand_in.wait()
    block = iota((8, SLOTS), 0)
    allowed = jnp.zeros((8, SLOTS), jnp.bool_)
    wide_cluster = lax.div(iota((8, SLOTS), 1), CAP)
    for cluster in range(PER_GROUP):
        for j in range(LISTED):
            listed = cand[j, g * PER_GROUP + cluster]
            allowed = allowed | ((block == listed) & (wide_cluster == cluster))
    penalty = jnp.where(allowed, 0.0, FAR)

    arrived(pool.at[0:12], ag2_recv)
    arrived(rxf.at[1:GROUPS], flag_sem.at[1])

    for b in range(8):
        rows = pool[2 * b : 2 * b + 2].reshape(BLK, WIDTH).astype(F32)
        square = jnp.sum(rows * rows, axis=1, keepdims=True)
        norms[b] = square + penalty[b : b + 1]

    def score(number, pair):
        first = max(pair[0], 1)
        arrived(rx.at[first : pair[-1] + 1], row_recv.at[number])
        rows = rx[pair[0] : pair[-1] + 1].reshape(len(pair) * SLOTS, WIDTH)
        live = jnp.concatenate([rxf[k, 0:1] for k in pair], axis=1)

        wide = len(pair) * SLOTS
        top = jnp.full((1, wide), -jnp.inf, F32)
        for t in range(4):
            tile = pool[4 * t : 4 * t + 4].reshape(4 * SHARD, WIDTH)
            inner = lax.dot_general(
                tile, rows, (((1,), (1,)), ((), ())), preferred_element_type=F32
            )
            square = norms[2 * t : 2 * t + 2].reshape(4 * SHARD, SLOTS)
            square = jnp.concatenate([square] * len(pair), axis=1)
            value = (2.0 * inner - square) * (1.0 / SOFTMAX_TEMP)
            logits[t, :, :wide] = value
            top = jnp.maximum(top, jnp.max(value, axis=0, keepdims=True))
        total = jnp.zeros((1, wide), F32)
        for t in range(4):
            value = jnp.exp(logits[t, :, :wide] - top)
            logits[t, :, :wide] = value
            total = total + jnp.sum(value, axis=0, keepdims=True)
        scale = live / total
        for t in range(4):
            value = (logits[t, :, :wide] * scale).astype(BF16).reshape(4, SHARD, wide)
            weights[4 * t : 4 * t + 4, :, pair[0] * SLOTS : (pair[-1] + 1) * SLOTS] = value
        affinity = SOFTMAX_TEMP * (top + jnp.log(total))
        for i, k in enumerate(pair):
            mine = jnp.broadcast_to(affinity[:, i * SLOTS : (i + 1) * SLOTS], (8, SLOTS))
            if k:
                afftx[k] = mine
                aff_copy(k).start()
            else:
                affrx[0] = mine

    for number, pair in enumerate(BATCHES):
        score(number, pair)

    part = (part_a, part_b)
    own = (own_a, own_b)
    far_in, near_in = (far_a, far_b), (near_a, near_b)
    send, last = (send_a, send_b), (last_a, last_b)

    def product(axis, index):
        lhs = jnp.concatenate([weights[member(index, i, axis)] for i in range(4)], axis=0)
        rhs = rx[:, :, axis * HALF : (axis + 1) * HALF].reshape(GROUPS * SLOTS, HALF)
        return jnp.dot(lhs, rhs, preferred_element_type=F32).reshape(4, SHARD, HALF)

    def span_of(sub):
        return pl.ds(SPANS[sub][0], SPANS[sub][1] - SPANS[sub][0])

    def hop(axis, sub, side, near, piece):
        first, second = place[axis]
        step = 1 - 2 * side
        span = pl.ds(piece * QUARTER, QUARTER)
        source = part[axis].at[turn(first, step if near else 2), span_of(sub), :, span]
        target = (g, member(turn(first, step), second, axis))
        if near:
            landing = near_in[axis].at[side, span_of(sub), :, span]
            return remote(source, landing, part_send.at[axis], near_recv.at[axis, sub], target)
        landing = far_in[axis].at[side, span_of(sub)]
        return remote(source, landing, part_send.at[axis], far_recv.at[axis, sub], target)

    def far(axis, sub):
        for side in (0, 1):
            hop(axis, sub, side, False, side).start()

    def direct(axis, sub):
        for side in (0, 1):
            hop(axis, sub, side, True, 1 - side).start()

    def relay(axis, sub):
        low, high = SPANS[sub]
        arrived(far_in[axis].at[:, span_of(sub)], far_recv.at[axis, sub])
        for side in (0, 1):
            index = turn(place[axis][0], 1 - 2 * side)
            span = slice(side * QUARTER, (side + 1) * QUARTER)
            part[axis][index, low:high, :, span] = (
                part[axis][index, low:high, :, span].astype(F32)
                + far_in[axis][side, low:high].astype(F32)
            ).astype(BF16)
            hop(axis, sub, side, True, side).start()

    def final(axis, sub):
        first, second = place[axis]
        low, high = SPANS[sub]
        arrived(near_in[axis].at[:, span_of(sub)], near_recv.at[axis, sub])
        total = own[axis][low:high]
        for side in (0, 1):
            total = total + near_in[axis][side, low:high].astype(F32)
        own[axis][low:high] = total
        send[axis][low:high] = total.astype(BF16)
        for holder in range(low, high):

            @pl.when(second != holder)
            def _():
                remote(
                    send[axis].at[holder],
                    last[axis].at[turn(second, -holder) - 1],
                    last_send.at[axis],
                    last_recv.at[axis],
                    (g, member(first, holder, axis)),
                ).start()

    for axis in (0, 1):
        index = turn(place[axis][0], 2)
        part[axis][index] = product(axis, index).astype(BF16)
        for sub in range(SUBS):
            far(axis, sub)
    for axis in (0, 1):
        for side in (0, 1):
            index = turn(place[axis][0], 1 - 2 * side)
            part[axis][index] = product(axis, index).astype(BF16)
        for sub in range(SUBS):
            direct(axis, sub)
    for axis in (0, 1):
        own[axis][...] = product(axis, place[axis][0])

    lanes = iota((SHARD, BLK), 1)
    diagonal = lanes == iota((SHARD, BLK), 0)

    def total1(k):
        to = turn(z, k)
        return remote(tot1.at[to], tot1rx.at[k], tot_sem.at[0], tot_sem.at[1], (g, to * 4 + y))

    def total2(k):
        to = turn(y, k)
        return remote(tot2.at[to], tot2rx.at[k], tot_sem.at[2], tot_sem.at[3], (g, z * 4 + to))

    def total_of(i, carry):
        for j in range(4):
            column = jnp.sum(weights[4 * i + j].astype(F32), axis=1, keepdims=True)
            row = jnp.sum(jnp.where(diagonal, column, 0.0), axis=0, keepdims=True)
            tot1[i, j] = jnp.broadcast_to(row, (8, BLK))
        return carry

    lax.fori_loop(0, 4, total_of, 0)

    for axis in (0, 1):
        relay(axis, 0)
    for axis in (0, 1):
        relay(axis, 1)
    for k in range(1, 4):
        total1(k).start()
    for axis in (0, 1):
        relay(axis, 2)
    for axis in (0, 1):
        final(axis, 0)
    arrived(tot1rx.at[1:4], tot_sem.at[1])
    totals = tot1[z]
    for k in range(1, 4):
        totals = totals + tot1rx[k]
    tot2[...] = totals
    for k in range(1, 4):
        total2(k).start()
    for axis in (0, 1):
        final(axis, 1)
    for axis in (0, 1):
        final(axis, 2)

    affinity = jnp.zeros((1, ROWS), F32)
    square_eye = iota((SLOTS, SLOTS), 0) == iota((SLOTS, SLOTS), 1)
    arrived(affrx.at[1:GROUPS], aff_sem.at[1])
    for k in range(GROUPS):
        column = jnp.sum(jnp.where(square_eye, affrx[k, 0:1], 0.0), axis=1, keepdims=True)
        here = slot == (slot_ids + group_at(k) * SLOTS).astype(F32)
        affinity = affinity + jnp.sum(jnp.where(here, column, 0.0), axis=0, keepdims=True)
    aff_ref[...] = affinity.reshape(ROWS)

    totals = tot2[y]
    arrived(tot2rx.at[1:4], tot_sem.at[3])
    for k in range(1, 4):
        totals = totals + tot2rx[k]
    column = jnp.sum(jnp.where(diagonal, totals[0:1], 0.0), axis=1, keepdims=True) + PRIOR_WEIGHT

    for axis in (0, 1):
        second = place[axis][1]
        total = own[axis][second]
        arrived(last[axis], last_recv.at[axis])
        for k in range(3):
            total = total + last[axis][k].astype(F32)
        span = slice(axis * HALF, (axis + 1) * HALF)
        prior = pool[d, :, span].astype(F32)
        new_ref[:, span] = (total + PRIOR_WEIGHT * prior) / column

    left(tx.at[1:GROUPS], row_send)
    left(txf.at[1:GROUPS], flag_sem.at[0])
    left(afftx.at[1:GROUPS], aff_sem.at[0])
    left(tot1.at[0:3], tot_sem.at[0])
    left(tot2.at[0:3], tot_sem.at[2])
    left(pool.at[0:15], ag_send)
    for axis in (0, 1):
        left(part[axis].at[0:3], part_send.at[axis])
        left(last[axis], last_send.at[axis])


def local(points, coarse, candidates, centroids):
    operands = (candidates.T, points, coarse.reshape(1, ROWS), centroids)
    vmem = pl.BlockSpec(memory_space=pltpu.VMEM)
    anywhere = pl.BlockSpec(memory_space=pl.ANY)
    dma = pltpu.SemaphoreType.DMA
    updated, affinity = pl.pallas_call(
        kernel,
        out_shape=(
            jax.ShapeDtypeStruct((SHARD, WIDTH), F32),
            jax.ShapeDtypeStruct((ROWS,), F32),
        ),
        in_specs=[anywhere] * 4,
        out_specs=(vmem, vmem),
        scratch_shapes=[
            pltpu.SMEM((LISTED, CLUSTERS), jnp.int32),
            pltpu.VMEM((ROWS, WIDTH), BF16),
            pltpu.VMEM((1, ROWS), jnp.int32),
            pltpu.VMEM((GROUPS, SLOTS, WIDTH), BF16),
            pltpu.VMEM((GROUPS, SLOTS, WIDTH), BF16),
            pltpu.VMEM((GROUPS, 8, SLOTS), F32),
            pltpu.VMEM((GROUPS, 8, SLOTS), F32),
            pltpu.VMEM((MEMBERS, SHARD, WIDTH), BF16),
            pltpu.VMEM((8, BLK, SLOTS), F32),
            pltpu.VMEM((4, 4 * SHARD, 2 * SLOTS), F32),
            pltpu.VMEM((MEMBERS, SHARD, GROUPS * SLOTS), BF16),
            pltpu.VMEM((GROUPS, 8, SLOTS), F32),
            pltpu.VMEM((GROUPS, 8, SLOTS), F32),
            pltpu.VMEM((4, 4, 8, BLK), F32),
            pltpu.VMEM((4, 4, 8, BLK), F32),
            pltpu.VMEM((4, 8, BLK), F32),
            pltpu.VMEM((4, 8, BLK), F32),
            pltpu.VMEM((4, 4, SHARD, HALF), BF16),
            pltpu.VMEM((4, 4, SHARD, HALF), BF16),
            pltpu.VMEM((4, SHARD, HALF), F32),
            pltpu.VMEM((4, SHARD, HALF), F32),
            pltpu.VMEM((2, 4, SHARD, QUARTER), BF16),
            pltpu.VMEM((2, 4, SHARD, QUARTER), BF16),
            pltpu.VMEM((2, 4, SHARD, HALF), BF16),
            pltpu.VMEM((2, 4, SHARD, HALF), BF16),
            pltpu.VMEM((4, SHARD, HALF), BF16),
            pltpu.VMEM((4, SHARD, HALF), BF16),
            pltpu.VMEM((3, SHARD, HALF), BF16),
            pltpu.VMEM((3, SHARD, HALF), BF16),
            dma((4,)),
            dma,
            dma((len(BATCHES),)),
            dma((2,)),
            dma((2,)),
            dma((4,)),
            dma,
            dma((2, 3)),
            dma,
            dma((2,)),
            dma((2, SUBS)),
            dma((2, SUBS)),
            dma((2,)),
            dma((2,)),
        ],
        compiler_params=pltpu.CompilerParams(
            collective_id=0, has_side_effects=True, vmem_limit_bytes=32 << 20
        ),
    )(*(pltpu.with_memory_space_constraint(a, pltpu.HBM) for a in operands))
    return updated, affinity


def solution(mesh):
    return jax.shard_map(
        local,
        mesh=mesh,
        in_specs=(P(("grp", "dev"), None), P(("grp", "dev"), None), P(), P(("grp", "dev"), None)),
        out_specs=(P(("grp", "dev"), None), P(("grp", "dev"))),
        check_vma=False,
    )
```

```python
import jax
import jax.numpy as jnp
from jax import lax
from jax.experimental import pallas as pl
from jax.experimental.pallas import tpu as pltpu
from jax.sharding import PartitionSpec as P

MESH = pl.DeviceIdType.MESH
F32 = jnp.float32
BF16 = jnp.bfloat16

SOFTMAX_TEMP = 0.4
PRIOR_WEIGHT = 1.0
FAR = 1e30

GROUPS = 8
MEMBERS = 16
ROWS = 512
WIDTH = 1024
SHARD = 64
POOL = MEMBERS * SHARD
PER_GROUP = 4
CLUSTERS = 32
CAP = 32
LISTED = 4
BLK = 128
SLOTS = PER_GROUP * CAP
HALF = WIDTH // 2
QUARTER = WIDTH // 4
SPANS = ((0, 1), (1, 2), (2, 4))
SUBS = len(SPANS)
EARLY = 6
AWAY = ((0, 0), (0, 1), (1, 0), (3, 0), (1, 1), (3, 1), (2, 0), (2, 1))
ORDER = (2, 3, 4, 5, 6, 7, 1)
BATCHES = ((0, 1), (2, 3), (4, 5), (6,), (7,))
LAST = GROUPS - 1


def iota(shape, axis):
    return lax.broadcasted_iota(jnp.int32, shape, axis)


def kernel(
    cand_hbm,
    points_hbm,
    coarse_hbm,
    cent_hbm,
    new_ref,
    aff_ref,
    cand,
    points,
    coarse,
    tx,
    rx,
    txf,
    rxf,
    pool,
    norms,
    logits,
    weights,
    afftx,
    affrx,
    tot1,
    tot1rx,
    tot2,
    tot2rx,
    part_a,
    part_b,
    acc_a,
    acc_b,
    early,
    own_a,
    own_b,
    far_a,
    far_b,
    near_a,
    near_b,
    send_a,
    send_b,
    last_a,
    last_b,
    in_sem,
    row_send,
    row_recv,
    flag_sem,
    aff_sem,
    tot_sem,
    ag_send,
    ag1_recv,
    ag2_recv,
    part_send,
    far_recv,
    near_recv,
    last_send,
    last_recv,
):
    g = lax.axis_index("grp")
    d = lax.axis_index("dev")
    x, c = lax.div(g, 2), lax.rem(g, 2)
    z, y = lax.div(d, 4), lax.rem(d, 4)

    def group_at(k):
        return lax.rem(x + AWAY[k][0], 4) * 2 + lax.rem(c + AWAY[k][1], 2)

    def group_from(k):
        return lax.rem(x + 4 - AWAY[k][0], 4) * 2 + lax.rem(c + AWAY[k][1], 2)

    def turn(value, by):
        return lax.rem(value + by + 4, 4)

    def member(first, second, axis):
        return first * 4 + second if axis == 0 else second * 4 + first

    place = ((z, y), (y, z))

    def remote(src, dst, send_sem, recv_sem, device):
        return pltpu.make_async_remote_copy(
            src_ref=src,
            dst_ref=dst,
            send_sem=send_sem,
            recv_sem=recv_sem,
            device_id=device,
            device_id_type=MESH,
        )

    barrier = pltpu.get_barrier_semaphore()
    for k in range(1, GROUPS):
        pl.semaphore_signal(barrier, inc=1, device_id=(group_at(k), d), device_id_type=MESH)
    for axis in (0, 1):
        first, second = place[axis]
        for k in range(1, 4):
            pl.semaphore_signal(
                barrier,
                inc=1,
                device_id=(g, member(turn(first, k), second, axis)),
                device_id_type=MESH,
            )

    coarse_in = pltpu.make_async_copy(coarse_hbm, coarse, in_sem.at[0])
    points_in = pltpu.make_async_copy(points_hbm, points, in_sem.at[1])
    cent_in = pltpu.make_async_copy(cent_hbm, pool.at[d], in_sem.at[2])
    cand_in = pltpu.make_async_copy(cand_hbm, cand, in_sem.at[3])
    coarse_in.start()
    points_in.start()
    cent_in.start()
    cand_in.start()

    cluster_ids = iota((CLUSTERS, ROWS), 0)
    before = (iota((ROWS, ROWS), 0) < iota((ROWS, ROWS), 1)).astype(F32).astype(BF16)
    coarse_in.wait()
    named = (coarse[...] == cluster_ids).astype(F32)
    rank = jnp.dot(named.astype(BF16), before, preferred_element_type=F32)
    slot = jnp.sum(named * (rank + (cluster_ids * CAP).astype(F32)), axis=0, keepdims=True)
    count = jnp.sum(named, axis=1, keepdims=True)
    slot_ids = iota((SLOTS, ROWS), 0)
    lane = iota((CLUSTERS, SLOTS), 1)
    lane_cluster, lane_rank = lax.div(lane, CAP), lax.rem(lane, CAP)

    def flag(owner):
        mine = iota((CLUSTERS, SLOTS), 0) == lane_cluster + owner * PER_GROUP
        held = jnp.sum(jnp.where(mine, count, 0.0), axis=0, keepdims=True)
        live = (lane_rank[0:1].astype(F32) < held).astype(F32)
        return jnp.broadcast_to(live, (8, SLOTS))

    def pack(owner):
        here = slot == (slot_ids + owner * SLOTS).astype(F32)
        return jnp.dot(
            here.astype(F32).astype(BF16), points[...], preferred_element_type=F32
        ).astype(BF16)

    def columns(axis):
        return pl.ds(axis * HALF, HALF)

    def row_copy(k):
        number = [k in batch for batch in BATCHES].index(True)
        return remote(tx.at[k], rx.at[k], row_send, row_recv.at[number], (group_at(k), d))

    def last_row_copy(half):
        span = columns(half)
        return remote(
            tx.at[LAST, :, span],
            rx.at[LAST, :, span],
            row_send,
            row_recv.at[len(BATCHES) - 1 + half],
            (group_at(LAST), d),
        )

    def flag_copy(k):
        return remote(txf.at[k], rxf.at[k], flag_sem.at[0], flag_sem.at[1], (group_at(k), d))

    def aff_copy(k):
        return remote(afftx.at[k], affrx.at[k], aff_sem.at[0], aff_sem.at[1], (group_from(k), d))

    def arrived(ref, sem):
        remote(ref, ref, sem, sem, (g, d)).wait_recv()

    def left(ref, sem):
        remote(ref, ref, sem, sem, (g, d)).wait_send()

    def gather1(axis, k):
        first, second = place[axis]
        piece = pool.at[d, :, columns(axis)]
        return remote(
            piece,
            piece,
            ag_send,
            ag1_recv.at[axis, k - 1],
            (g, member(turn(first, k), second, axis)),
        )

    def gather2(axis, k1, k2):
        first, second = place[axis]
        piece = pool.at[member(turn(first, -k1), second, axis), :, columns(axis)]
        return remote(
            piece,
            piece,
            ag_send,
            ag2_recv,
            (g, member(first, turn(second, k2), axis)),
        )

    for k in ORDER:
        txf[k] = flag(group_at(k))
    rxf[0] = flag(g)
    points_in.wait()
    tx[ORDER[0]] = pack(group_at(ORDER[0]))
    pl.semaphore_wait(barrier, GROUPS - 1 + 6)
    for i, k in enumerate(ORDER):
        if i:
            tx[k] = pack(group_at(k))
        if k == LAST:
            last_row_copy(0).start()
            last_row_copy(1).start()
        else:
            row_copy(k).start()
        if i == 1:
            for k1 in ORDER:
                flag_copy(k1).start()
            cent_in.wait()
            for axis in (0, 1):
                for k1 in (2, 1, 3):
                    gather1(axis, k1).start()
        if i == 2:
            for axis in (0, 1):
                for k2 in (2, 1, 3):
                    gather2(axis, 0, k2).start()
    rx[0] = pack(g)

    for k1 in (1, 3, 2):
        for axis in (0, 1):
            gather1(axis, k1).wait_recv()
            for k2 in (2, 1, 3):
                gather2(axis, k1, k2).start()

    cand_in.wait()
    block = iota((8, SLOTS), 0)
    allowed = jnp.zeros((8, SLOTS), jnp.bool_)
    wide_cluster = lax.div(iota((8, SLOTS), 1), CAP)
    for cluster in range(PER_GROUP):
        for j in range(LISTED):
            listed = cand[j, g * PER_GROUP + cluster]
            allowed = allowed | ((block == listed) & (wide_cluster == cluster))
    penalty = jnp.where(allowed, 0.0, FAR)

    arrived(pool.at[0:12], ag2_recv)
    arrived(rxf.at[1:GROUPS], flag_sem.at[1])

    for b in range(8):
        rows = pool[2 * b : 2 * b + 2].reshape(BLK, WIDTH).astype(F32)
        square = jnp.sum(rows * rows, axis=1, keepdims=True)
        norms[b] = square + penalty[b : b + 1]

    def score(number, pair):
        if pair[0] == LAST:
            arrived(rx.at[LAST, :, columns(0)], row_recv.at[number])
        else:
            first = max(pair[0], 1)
            arrived(rx.at[first : pair[-1] + 1], row_recv.at[number])
        live = jnp.concatenate([rxf[k, 0:1] for k in pair], axis=1)

        wide = len(pair) * SLOTS

        def inner_products(t, span):
            return lax.dot_general(
                pool[4 * t : 4 * t + 4, :, span].reshape(4 * SHARD, -1),
                rx[pair[0] : pair[-1] + 1, :, span].reshape(wide, -1),
                (((1,), (1,)), ((), ())),
                preferred_element_type=F32,
            )

        if pair[0] == LAST:
            for t in range(4):
                logits[t, :, :wide] = inner_products(t, slice(0, HALF))
            arrived(rx.at[LAST, :, columns(1)], row_recv.at[number + 1])
        top = jnp.full((1, wide), -jnp.inf, F32)
        for t in range(4):
            if pair[0] == LAST:
                inner = logits[t, :, :wide] + inner_products(t, slice(HALF, WIDTH))
            else:
                inner = inner_products(t, slice(0, WIDTH))
            square = norms[2 * t : 2 * t + 2].reshape(4 * SHARD, SLOTS)
            square = jnp.concatenate([square] * len(pair), axis=1)
            value = (2.0 * inner - square) * (1.0 / SOFTMAX_TEMP)
            logits[t, :, :wide] = value
            top = jnp.maximum(top, jnp.max(value, axis=0, keepdims=True))
        total = jnp.zeros((1, wide), F32)
        for t in range(4):
            value = jnp.exp(logits[t, :, :wide] - top)
            logits[t, :, :wide] = value
            total = total + jnp.sum(value, axis=0, keepdims=True)
        scale = live / total
        for t in range(4):
            value = (logits[t, :, :wide] * scale).astype(BF16).reshape(4, SHARD, wide)
            weights[4 * t : 4 * t + 4, :, pair[0] * SLOTS : (pair[-1] + 1) * SLOTS] = value
        affinity = SOFTMAX_TEMP * (top + jnp.log(total))
        for i, k in enumerate(pair):
            mine = jnp.broadcast_to(affinity[:, i * SLOTS : (i + 1) * SLOTS], (8, SLOTS))
            if k:
                afftx[k] = mine
                aff_copy(k).start()
            else:
                affrx[0] = mine

    acc = (acc_a, acc_b)

    def partial(axis, index, low, high):
        lanes = slice(low * SLOTS, high * SLOTS)
        lhs = jnp.concatenate([weights[member(index, i, axis), :, lanes] for i in range(4)], axis=0)
        rhs = rx[low:high, :, axis * HALF : (axis + 1) * HALF].reshape((high - low) * SLOTS, HALF)
        return jnp.dot(lhs, rhs, preferred_element_type=F32).reshape(4, SHARD, HALF)

    def product(axis, index):
        return acc[axis][index] + partial(axis, index, EARLY, GROUPS)

    def lane_sums(i, low, high):
        total = weights[i, :, low * SLOTS : (low + 1) * SLOTS].astype(F32)
        for k in range(low + 1, high):
            total = total + weights[i, :, k * SLOTS : (k + 1) * SLOTS].astype(F32)
        return total

    def early_sums(i, carry):
        early[i] = lane_sums(i, 0, EARLY)
        return carry

    for number, pair in enumerate(BATCHES):
        if pair[0] == EARLY:
            for axis in (0, 1):
                for index in range(4):
                    acc[axis][index] = partial(axis, index, 0, EARLY)
            lax.fori_loop(0, MEMBERS, early_sums, 0)
        score(number, pair)

    part = (part_a, part_b)
    own = (own_a, own_b)
    far_in, near_in = (far_a, far_b), (near_a, near_b)
    send, last = (send_a, send_b), (last_a, last_b)

    def span_of(sub):
        return pl.ds(SPANS[sub][0], SPANS[sub][1] - SPANS[sub][0])

    def hop(axis, sub, side, near, piece):
        first, second = place[axis]
        step = 1 - 2 * side
        span = pl.ds(piece * QUARTER, QUARTER)
        source = part[axis].at[turn(first, step if near else 2), span_of(sub), :, span]
        target = (g, member(turn(first, step), second, axis))
        if near:
            landing = near_in[axis].at[side, span_of(sub), :, span]
            return remote(source, landing, part_send.at[axis], near_recv.at[axis, sub], target)
        landing = far_in[axis].at[side, span_of(sub)]
        return remote(source, landing, part_send.at[axis], far_recv.at[axis, sub], target)

    def far(axis, sub):
        for side in (0, 1):
            hop(axis, sub, side, False, side).start()

    def direct(axis, sub):
        for side in (0, 1):
            hop(axis, sub, side, True, 1 - side).start()

    def relay(axis, sub):
        low, high = SPANS[sub]
        arrived(far_in[axis].at[:, span_of(sub)], far_recv.at[axis, sub])
        for side in (0, 1):
            index = turn(place[axis][0], 1 - 2 * side)
            span = slice(side * QUARTER, (side + 1) * QUARTER)
            part[axis][index, low:high, :, span] = (
                part[axis][index, low:high, :, span].astype(F32)
                + far_in[axis][side, low:high].astype(F32)
            ).astype(BF16)
            hop(axis, sub, side, True, side).start()

    def final(axis, sub):
        first, second = place[axis]
        low, high = SPANS[sub]
        arrived(near_in[axis].at[:, span_of(sub)], near_recv.at[axis, sub])
        total = own[axis][low:high]
        for side in (0, 1):
            total = total + near_in[axis][side, low:high].astype(F32)
        own[axis][low:high] = total
        send[axis][low:high] = total.astype(BF16)
        for holder in range(low, high):

            @pl.when(second != holder)
            def _():
                remote(
                    send[axis].at[holder],
                    last[axis].at[turn(second, -holder) - 1],
                    last_send.at[axis],
                    last_recv.at[axis],
                    (g, member(first, holder, axis)),
                ).start()

    for axis in (0, 1):
        index = turn(place[axis][0], 2)
        part[axis][index] = product(axis, index).astype(BF16)
        for sub in range(SUBS):
            far(axis, sub)
    for axis in (0, 1):
        for side in (0, 1):
            index = turn(place[axis][0], 1 - 2 * side)
            part[axis][index] = product(axis, index).astype(BF16)
        for sub in range(SUBS):
            direct(axis, sub)
    for axis in (0, 1):
        own[axis][...] = product(axis, place[axis][0])

    lanes = iota((SHARD, BLK), 1)
    diagonal = lanes == iota((SHARD, BLK), 0)

    def total1(k):
        to = turn(z, k)
        return remote(tot1.at[to], tot1rx.at[k], tot_sem.at[0], tot_sem.at[1], (g, to * 4 + y))

    def total2(k):
        to = turn(y, k)
        return remote(tot2.at[to], tot2rx.at[k], tot_sem.at[2], tot_sem.at[3], (g, z * 4 + to))

    def total_of(i, carry):
        for j in range(4):
            found = early[4 * i + j] + lane_sums(4 * i + j, EARLY, GROUPS)
            column = jnp.sum(found, axis=1, keepdims=True)
            row = jnp.sum(jnp.where(diagonal, column, 0.0), axis=0, keepdims=True)
            tot1[i, j] = jnp.broadcast_to(row, (8, BLK))
        return carry

    lax.fori_loop(0, 4, total_of, 0)

    for axis in (0, 1):
        relay(axis, 0)
    for axis in (0, 1):
        relay(axis, 1)
    for k in range(1, 4):
        total1(k).start()
    for axis in (0, 1):
        relay(axis, 2)
    for axis in (0, 1):
        final(axis, 0)
    arrived(tot1rx.at[1:4], tot_sem.at[1])
    totals = tot1[z]
    for k in range(1, 4):
        totals = totals + tot1rx[k]
    tot2[...] = totals
    for k in range(1, 4):
        total2(k).start()
    for axis in (0, 1):
        final(axis, 1)
    for axis in (0, 1):
        final(axis, 2)

    affinity = jnp.zeros((1, ROWS), F32)
    square_eye = iota((SLOTS, SLOTS), 0) == iota((SLOTS, SLOTS), 1)
    arrived(affrx.at[1:GROUPS], aff_sem.at[1])
    for k in range(GROUPS):
        column = jnp.sum(jnp.where(square_eye, affrx[k, 0:1], 0.0), axis=1, keepdims=True)
        here = slot == (slot_ids + group_at(k) * SLOTS).astype(F32)
        affinity = affinity + jnp.sum(jnp.where(here, column, 0.0), axis=0, keepdims=True)
    aff_ref[...] = affinity.reshape(ROWS)

    totals = tot2[y]
    arrived(tot2rx.at[1:4], tot_sem.at[3])
    for k in range(1, 4):
        totals = totals + tot2rx[k]
    column = jnp.sum(jnp.where(diagonal, totals[0:1], 0.0), axis=1, keepdims=True) + PRIOR_WEIGHT

    for axis in (0, 1):
        second = place[axis][1]
        total = own[axis][second]
        arrived(last[axis], last_recv.at[axis])
        for k in range(3):
            total = total + last[axis][k].astype(F32)
        span = slice(axis * HALF, (axis + 1) * HALF)
        prior = pool[d, :, span].astype(F32)
        new_ref[:, span] = (total + PRIOR_WEIGHT * prior) / column

    left(tx.at[1:GROUPS], row_send)
    left(txf.at[1:GROUPS], flag_sem.at[0])
    left(afftx.at[1:GROUPS], aff_sem.at[0])
    left(tot1.at[0:3], tot_sem.at[0])
    left(tot2.at[0:3], tot_sem.at[2])
    left(pool.at[0:15], ag_send)
    for axis in (0, 1):
        left(part[axis].at[0:3], part_send.at[axis])
        left(last[axis], last_send.at[axis])


def local(points, coarse, candidates, centroids):
    operands = (candidates.T, points, coarse.reshape(1, ROWS), centroids)
    vmem = pl.BlockSpec(memory_space=pltpu.VMEM)
    anywhere = pl.BlockSpec(memory_space=pl.ANY)
    dma = pltpu.SemaphoreType.DMA
    updated, affinity = pl.pallas_call(
        kernel,
        out_shape=(
            jax.ShapeDtypeStruct((SHARD, WIDTH), F32),
            jax.ShapeDtypeStruct((ROWS,), F32),
        ),
        in_specs=[anywhere] * 4,
        out_specs=(vmem, vmem),
        scratch_shapes=[
            pltpu.SMEM((LISTED, CLUSTERS), jnp.int32),
            pltpu.VMEM((ROWS, WIDTH), BF16),
            pltpu.VMEM((1, ROWS), jnp.int32),
            pltpu.VMEM((GROUPS, SLOTS, WIDTH), BF16),
            pltpu.VMEM((GROUPS, SLOTS, WIDTH), BF16),
            pltpu.VMEM((GROUPS, 8, SLOTS), F32),
            pltpu.VMEM((GROUPS, 8, SLOTS), F32),
            pltpu.VMEM((MEMBERS, SHARD, WIDTH), BF16),
            pltpu.VMEM((8, BLK, SLOTS), F32),
            pltpu.VMEM((4, 4 * SHARD, 2 * SLOTS), F32),
            pltpu.VMEM((MEMBERS, SHARD, GROUPS * SLOTS), BF16),
            pltpu.VMEM((GROUPS, 8, SLOTS), F32),
            pltpu.VMEM((GROUPS, 8, SLOTS), F32),
            pltpu.VMEM((4, 4, 8, BLK), F32),
            pltpu.VMEM((4, 4, 8, BLK), F32),
            pltpu.VMEM((4, 8, BLK), F32),
            pltpu.VMEM((4, 8, BLK), F32),
            pltpu.VMEM((4, 4, SHARD, HALF), BF16),
            pltpu.VMEM((4, 4, SHARD, HALF), BF16),
            pltpu.VMEM((4, 4, SHARD, HALF), F32),
            pltpu.VMEM((4, 4, SHARD, HALF), F32),
            pltpu.VMEM((MEMBERS, SHARD, BLK), F32),
            pltpu.VMEM((4, SHARD, HALF), F32),
            pltpu.VMEM((4, SHARD, HALF), F32),
            pltpu.VMEM((2, 4, SHARD, QUARTER), BF16),
            pltpu.VMEM((2, 4, SHARD, QUARTER), BF16),
            pltpu.VMEM((2, 4, SHARD, HALF), BF16),
            pltpu.VMEM((2, 4, SHARD, HALF), BF16),
            pltpu.VMEM((4, SHARD, HALF), BF16),
            pltpu.VMEM((4, SHARD, HALF), BF16),
            pltpu.VMEM((3, SHARD, HALF), BF16),
            pltpu.VMEM((3, SHARD, HALF), BF16),
            dma((4,)),
            dma,
            dma((len(BATCHES) + 1,)),
            dma((2,)),
            dma((2,)),
            dma((4,)),
            dma,
            dma((2, 3)),
            dma,
            dma((2,)),
            dma((2, SUBS)),
            dma((2, SUBS)),
            dma((2,)),
            dma((2,)),
        ],
        compiler_params=pltpu.CompilerParams(
            collective_id=0, has_side_effects=True, vmem_limit_bytes=32 << 20
        ),
    )(*(pltpu.with_memory_space_constraint(a, pltpu.HBM) for a in operands))
    return updated, affinity


def solution(mesh):
    return jax.shard_map(
        local,
        mesh=mesh,
        in_specs=(P(("grp", "dev"), None), P(("grp", "dev"), None), P(), P(("grp", "dev"), None)),
        out_specs=(P(("grp", "dev"), None), P(("grp", "dev"))),
        check_vma=False,
    )
```

```python
import jax
import jax.numpy as jnp
from jax import lax
from jax.experimental import pallas as pl
from jax.experimental.pallas import tpu as pltpu
from jax.sharding import PartitionSpec as P

MESH = pl.DeviceIdType.MESH
F32 = jnp.float32
BF16 = jnp.bfloat16

SOFTMAX_TEMP = 0.4
PRIOR_WEIGHT = 1.0
FAR = 1e30

GROUPS = 8
MEMBERS = 16
ROWS = 512
WIDTH = 1024
SHARD = 64
POOL = MEMBERS * SHARD
PER_GROUP = 4
CLUSTERS = 32
CAP = 32
LISTED = 4
BLK = 128
SLOTS = PER_GROUP * CAP
HALF = WIDTH // 2
QUARTER = WIDTH // 4
SPANS = ((0, 1), (1, 2), (2, 4))
SUBS = len(SPANS)
EARLY = 6
AWAY = ((0, 0), (0, 1), (1, 0), (3, 0), (1, 1), (3, 1), (2, 0), (2, 1))
ORDER = (2, 3, 4, 5, 6, 7, 1)
BATCHES = ((0, 1), (2, 3), (4, 5), (6,), (7,))
LAST = GROUPS - 1


def iota(shape, axis):
    return lax.broadcasted_iota(jnp.int32, shape, axis)


def kernel(
    cand_hbm,
    points_hbm,
    coarse_hbm,
    cent_hbm,
    new_ref,
    aff_ref,
    cand,
    points,
    coarse,
    tx,
    rx,
    txf,
    rxf,
    pool,
    norms,
    logits,
    weights,
    afftx,
    affrx,
    tot1,
    tot1rx,
    tot2,
    tot2rx,
    part_a,
    part_b,
    acc_a,
    acc_b,
    early,
    own_a,
    own_b,
    far_a,
    far_b,
    near_a,
    near_b,
    send_a,
    send_b,
    last_a,
    last_b,
    in_sem,
    row_send,
    row_recv,
    flag_sem,
    aff_sem,
    tot_sem,
    ag_send,
    ag1_recv,
    ag2_recv,
    part_send,
    far_recv,
    near_recv,
    last_send,
    last_recv,
):
    g = lax.axis_index("grp")
    d = lax.axis_index("dev")
    x, c = lax.div(g, 2), lax.rem(g, 2)
    z, y = lax.div(d, 4), lax.rem(d, 4)

    def group_at(k):
        return lax.rem(x + AWAY[k][0], 4) * 2 + lax.rem(c + AWAY[k][1], 2)

    def group_from(k):
        return lax.rem(x + 4 - AWAY[k][0], 4) * 2 + lax.rem(c + AWAY[k][1], 2)

    def turn(value, by):
        return lax.rem(value + by + 4, 4)

    def member(first, second, axis):
        return first * 4 + second if axis == 0 else second * 4 + first

    place = ((z, y), (y, z))

    def remote(src, dst, send_sem, recv_sem, device):
        return pltpu.make_async_remote_copy(
            src_ref=src,
            dst_ref=dst,
            send_sem=send_sem,
            recv_sem=recv_sem,
            device_id=device,
            device_id_type=MESH,
        )

    coarse_in = pltpu.make_async_copy(coarse_hbm, coarse, in_sem.at[0])
    points_in = pltpu.make_async_copy(points_hbm, points, in_sem.at[1])
    coarse_in.start()
    points_in.start()

    barrier = pltpu.get_barrier_semaphore()
    for k in range(1, GROUPS):
        pl.semaphore_signal(barrier, inc=1, device_id=(group_at(k), d), device_id_type=MESH)
    for axis in (0, 1):
        first, second = place[axis]
        for k in range(1, 4):
            pl.semaphore_signal(
                barrier,
                inc=1,
                device_id=(g, member(turn(first, k), second, axis)),
                device_id_type=MESH,
            )

    cent_in = pltpu.make_async_copy(cent_hbm, pool.at[d], in_sem.at[2])
    cand_in = pltpu.make_async_copy(cand_hbm, cand, in_sem.at[3])
    cent_in.start()
    cand_in.start()

    cluster_ids = iota((CLUSTERS, ROWS), 0)
    before = (iota((ROWS, ROWS), 0) < iota((ROWS, ROWS), 1)).astype(F32).astype(BF16)
    coarse_in.wait()
    named = (coarse[...] == cluster_ids).astype(F32)
    rank = jnp.dot(named.astype(BF16), before, preferred_element_type=F32)
    slot = jnp.sum(named * (rank + (cluster_ids * CAP).astype(F32)), axis=0, keepdims=True)
    count = jnp.sum(named, axis=1, keepdims=True)
    slot_ids = iota((SLOTS, ROWS), 0)
    lane = iota((CLUSTERS, SLOTS), 1)
    lane_cluster, lane_rank = lax.div(lane, CAP), lax.rem(lane, CAP)

    def flag(owner):
        mine = iota((CLUSTERS, SLOTS), 0) == lane_cluster + owner * PER_GROUP
        held = jnp.sum(jnp.where(mine, count, 0.0), axis=0, keepdims=True)
        live = (lane_rank[0:1].astype(F32) < held).astype(F32)
        return jnp.broadcast_to(live, (8, SLOTS))

    def pack(owner):
        here = slot == (slot_ids + owner * SLOTS).astype(F32)
        return jnp.dot(
            here.astype(F32).astype(BF16), points[...], preferred_element_type=F32
        ).astype(BF16)

    def columns(axis):
        return pl.ds(axis * HALF, HALF)

    def row_copy(k):
        number = [k in batch for batch in BATCHES].index(True)
        return remote(tx.at[k], rx.at[k], row_send, row_recv.at[number], (group_at(k), d))

    def last_row_copy(half):
        span = columns(half)
        return remote(
            tx.at[LAST, :, span],
            rx.at[LAST, :, span],
            row_send,
            row_recv.at[len(BATCHES) - 1 + half],
            (group_at(LAST), d),
        )

    def flag_copy(k):
        return remote(txf.at[k], rxf.at[k], flag_sem.at[0], flag_sem.at[1], (group_at(k), d))

    def aff_copy(k):
        return remote(afftx.at[k], affrx.at[k], aff_sem.at[0], aff_sem.at[1], (group_from(k), d))

    def arrived(ref, sem):
        remote(ref, ref, sem, sem, (g, d)).wait_recv()

    def left(ref, sem):
        remote(ref, ref, sem, sem, (g, d)).wait_send()

    def gather1(axis, k):
        first, second = place[axis]
        piece = pool.at[d, :, columns(axis)]
        return remote(
            piece,
            piece,
            ag_send,
            ag1_recv.at[axis, k - 1],
            (g, member(turn(first, k), second, axis)),
        )

    def gather2(axis, k1, k2):
        first, second = place[axis]
        piece = pool.at[member(turn(first, -k1), second, axis), :, columns(axis)]
        return remote(
            piece,
            piece,
            ag_send,
            ag2_recv,
            (g, member(first, turn(second, k2), axis)),
        )

    for k in ORDER:
        txf[k] = flag(group_at(k))
    rxf[0] = flag(g)
    points_in.wait()
    tx[ORDER[0]] = pack(group_at(ORDER[0]))
    pl.semaphore_wait(barrier, GROUPS - 1 + 6)
    for i, k in enumerate(ORDER):
        if i:
            tx[k] = pack(group_at(k))
        if k == LAST:
            last_row_copy(0).start()
            last_row_copy(1).start()
        else:
            row_copy(k).start()
        if i == 1:
            for k1 in ORDER:
                flag_copy(k1).start()
            cent_in.wait()
            for axis in (0, 1):
                for k1 in (2, 1, 3):
                    gather1(axis, k1).start()
        if i == 2:
            for axis in (0, 1):
                for k2 in (2, 1, 3):
                    gather2(axis, 0, k2).start()
    rx[0] = pack(g)

    for k1 in (1, 3, 2):
        for axis in (0, 1):
            gather1(axis, k1).wait_recv()
            for k2 in (2, 1, 3):
                gather2(axis, k1, k2).start()

    cand_in.wait()
    block = iota((8, SLOTS), 0)
    allowed = jnp.zeros((8, SLOTS), jnp.bool_)
    wide_cluster = lax.div(iota((8, SLOTS), 1), CAP)
    for cluster in range(PER_GROUP):
        for j in range(LISTED):
            listed = cand[j, g * PER_GROUP + cluster]
            allowed = allowed | ((block == listed) & (wide_cluster == cluster))
    penalty = jnp.where(allowed, 0.0, FAR)

    arrived(pool.at[0:12], ag2_recv)
    arrived(rxf.at[1:GROUPS], flag_sem.at[1])

    for b in range(8):
        rows = pool[2 * b : 2 * b + 2].reshape(BLK, WIDTH).astype(F32)
        square = jnp.sum(rows * rows, axis=1, keepdims=True)
        norms[b] = square + penalty[b : b + 1]

    def score(number, pair):
        if pair[0] == LAST:
            arrived(rx.at[LAST, :, columns(0)], row_recv.at[number])
        else:
            first = max(pair[0], 1)
            arrived(rx.at[first : pair[-1] + 1], row_recv.at[number])
        live = jnp.concatenate([rxf[k, 0:1] for k in pair], axis=1)

        wide = len(pair) * SLOTS

        def inner_products(t, span):
            return lax.dot_general(
                pool[4 * t : 4 * t + 4, :, span].reshape(4 * SHARD, -1),
                rx[pair[0] : pair[-1] + 1, :, span].reshape(wide, -1),
                (((1,), (1,)), ((), ())),
                preferred_element_type=F32,
            )

        if pair[0] == LAST:
            for t in range(4):
                logits[t, :, :wide] = inner_products(t, slice(0, HALF))
            arrived(rx.at[LAST, :, columns(1)], row_recv.at[number + 1])
        top = jnp.full((1, wide), -jnp.inf, F32)
        for t in range(4):
            if pair[0] == LAST:
                inner = logits[t, :, :wide] + inner_products(t, slice(HALF, WIDTH))
            else:
                inner = inner_products(t, slice(0, WIDTH))
            square = norms[2 * t : 2 * t + 2].reshape(4 * SHARD, SLOTS)
            square = jnp.concatenate([square] * len(pair), axis=1)
            value = (2.0 * inner - square) * (1.0 / SOFTMAX_TEMP)
            logits[t, :, :wide] = value
            top = jnp.maximum(top, jnp.max(value, axis=0, keepdims=True))
        total = jnp.zeros((1, wide), F32)
        for t in range(4):
            value = jnp.exp(logits[t, :, :wide] - top)
            logits[t, :, :wide] = value
            total = total + jnp.sum(value, axis=0, keepdims=True)
        scale = live / total
        for t in range(4):
            value = (logits[t, :, :wide] * scale).astype(BF16).reshape(4, SHARD, wide)
            weights[4 * t : 4 * t + 4, :, pair[0] * SLOTS : (pair[-1] + 1) * SLOTS] = value
        affinity = SOFTMAX_TEMP * (top + jnp.log(total))
        for i, k in enumerate(pair):
            mine = jnp.broadcast_to(affinity[:, i * SLOTS : (i + 1) * SLOTS], (8, SLOTS))
            if k:
                afftx[k] = mine
                aff_copy(k).start()
            else:
                affrx[0] = mine

    acc = (acc_a, acc_b)

    def partial(axis, index, low, high):
        lanes = slice(low * SLOTS, high * SLOTS)
        lhs = jnp.concatenate([weights[member(index, i, axis), :, lanes] for i in range(4)], axis=0)
        rhs = rx[low:high, :, axis * HALF : (axis + 1) * HALF].reshape((high - low) * SLOTS, HALF)
        return jnp.dot(lhs, rhs, preferred_element_type=F32).reshape(4, SHARD, HALF)

    def product(axis, index):
        return acc[axis][index] + partial(axis, index, EARLY, GROUPS)

    def lane_sums(i, low, high):
        total = weights[i, :, low * SLOTS : (low + 1) * SLOTS].astype(F32)
        for k in range(low + 1, high):
            total = total + weights[i, :, k * SLOTS : (k + 1) * SLOTS].astype(F32)
        return total

    def early_sums(i, carry):
        early[i] = lane_sums(i, 0, EARLY)
        return carry

    for number, pair in enumerate(BATCHES):
        if pair[0] == EARLY:
            for axis in (0, 1):
                for index in range(4):
                    acc[axis][index] = partial(axis, index, 0, EARLY)
            lax.fori_loop(0, MEMBERS, early_sums, 0)
        score(number, pair)

    part = (part_a, part_b)
    own = (own_a, own_b)
    far_in, near_in = (far_a, far_b), (near_a, near_b)
    send, last = (send_a, send_b), (last_a, last_b)

    def span_of(sub):
        return pl.ds(SPANS[sub][0], SPANS[sub][1] - SPANS[sub][0])

    def hop(axis, sub, side, near, piece):
        first, second = place[axis]
        step = 1 - 2 * side
        span = pl.ds(piece * QUARTER, QUARTER)
        source = part[axis].at[turn(first, step if near else 2), span_of(sub), :, span]
        target = (g, member(turn(first, step), second, axis))
        if near:
            landing = near_in[axis].at[side, span_of(sub), :, span]
            return remote(source, landing, part_send.at[axis], near_recv.at[axis, sub], target)
        landing = far_in[axis].at[side, span_of(sub)]
        return remote(source, landing, part_send.at[axis], far_recv.at[axis, sub], target)

    def far(axis, sub):
        for side in (0, 1):
            hop(axis, sub, side, False, side).start()

    def direct(axis, sub):
        for side in (0, 1):
            hop(axis, sub, side, True, 1 - side).start()

    def relay(axis, sub):
        low, high = SPANS[sub]
        arrived(far_in[axis].at[:, span_of(sub)], far_recv.at[axis, sub])
        for side in (0, 1):
            index = turn(place[axis][0], 1 - 2 * side)
            span = slice(side * QUARTER, (side + 1) * QUARTER)
            part[axis][index, low:high, :, span] = (
                part[axis][index, low:high, :, span].astype(F32)
                + far_in[axis][side, low:high].astype(F32)
            ).astype(BF16)
            hop(axis, sub, side, True, side).start()

    def final(axis, sub):
        first, second = place[axis]
        low, high = SPANS[sub]
        arrived(near_in[axis].at[:, span_of(sub)], near_recv.at[axis, sub])
        total = own[axis][low:high]
        for side in (0, 1):
            total = total + near_in[axis][side, low:high].astype(F32)
        own[axis][low:high] = total
        send[axis][low:high] = total.astype(BF16)
        for holder in range(low, high):

            @pl.when(second != holder)
            def _():
                remote(
                    send[axis].at[holder],
                    last[axis].at[turn(second, -holder) - 1],
                    last_send.at[axis],
                    last_recv.at[axis],
                    (g, member(first, holder, axis)),
                ).start()

    for axis in (0, 1):
        index = turn(place[axis][0], 2)
        part[axis][index] = product(axis, index).astype(BF16)
        for sub in range(SUBS):
            far(axis, sub)
    for axis in (0, 1):
        for side in (0, 1):
            index = turn(place[axis][0], 1 - 2 * side)
            part[axis][index] = product(axis, index).astype(BF16)
        for sub in range(SUBS):
            direct(axis, sub)
    for axis in (0, 1):
        own[axis][...] = product(axis, place[axis][0])

    lanes = iota((SHARD, BLK), 1)
    diagonal = lanes == iota((SHARD, BLK), 0)

    def total1(k):
        to = turn(z, k)
        return remote(tot1.at[to], tot1rx.at[k], tot_sem.at[0], tot_sem.at[1], (g, to * 4 + y))

    def total2(k):
        to = turn(y, k)
        return remote(tot2.at[to], tot2rx.at[k], tot_sem.at[2], tot_sem.at[3], (g, z * 4 + to))

    def total_of(i, carry):
        for j in range(4):
            found = early[4 * i + j] + lane_sums(4 * i + j, EARLY, GROUPS)
            column = jnp.sum(found, axis=1, keepdims=True)
            row = jnp.sum(jnp.where(diagonal, column, 0.0), axis=0, keepdims=True)
            tot1[i, j] = jnp.broadcast_to(row, (8, BLK))
        return carry

    lax.fori_loop(0, 4, total_of, 0)

    for axis in (0, 1):
        relay(axis, 0)
    for axis in (0, 1):
        relay(axis, 1)
    for k in range(1, 4):
        total1(k).start()
    for axis in (0, 1):
        relay(axis, 2)
    for axis in (0, 1):
        final(axis, 0)
    arrived(tot1rx.at[1:4], tot_sem.at[1])
    totals = tot1[z]
    for k in range(1, 4):
        totals = totals + tot1rx[k]
    tot2[...] = totals
    for k in range(1, 4):
        total2(k).start()
    for axis in (0, 1):
        final(axis, 1)
    for axis in (0, 1):
        final(axis, 2)

    affinity = jnp.zeros((1, ROWS), F32)
    square_eye = iota((SLOTS, SLOTS), 0) == iota((SLOTS, SLOTS), 1)
    arrived(affrx.at[1:GROUPS], aff_sem.at[1])
    for k in range(GROUPS):
        column = jnp.sum(jnp.where(square_eye, affrx[k, 0:1], 0.0), axis=1, keepdims=True)
        here = slot == (slot_ids + group_at(k) * SLOTS).astype(F32)
        affinity = affinity + jnp.sum(jnp.where(here, column, 0.0), axis=0, keepdims=True)
    aff_ref[...] = affinity.reshape(ROWS)

    totals = tot2[y]
    arrived(tot2rx.at[1:4], tot_sem.at[3])
    for k in range(1, 4):
        totals = totals + tot2rx[k]
    column = jnp.sum(jnp.where(diagonal, totals[0:1], 0.0), axis=1, keepdims=True) + PRIOR_WEIGHT
    scale = 1.0 / column

    for axis in (0, 1):
        second = place[axis][1]
        span = slice(axis * HALF, (axis + 1) * HALF)
        total = own[axis][second] + PRIOR_WEIGHT * pool[d, :, span].astype(F32)
        arrived(last[axis], last_recv.at[axis])
        for k in range(3):
            total = total + last[axis][k].astype(F32)
        new_ref[:, span] = total * scale

    left(tx.at[1:GROUPS], row_send)
    left(txf.at[1:GROUPS], flag_sem.at[0])
    left(afftx.at[1:GROUPS], aff_sem.at[0])
    left(tot1.at[0:3], tot_sem.at[0])
    left(tot2.at[0:3], tot_sem.at[2])
    left(pool.at[0:15], ag_send)
    for axis in (0, 1):
        left(part[axis].at[0:3], part_send.at[axis])
        left(last[axis], last_send.at[axis])


def local(points, coarse, candidates, centroids):
    operands = (candidates.T, points, coarse.reshape(1, ROWS), centroids)
    vmem = pl.BlockSpec(memory_space=pltpu.VMEM)
    anywhere = pl.BlockSpec(memory_space=pl.ANY)
    dma = pltpu.SemaphoreType.DMA
    updated, affinity = pl.pallas_call(
        kernel,
        out_shape=(
            jax.ShapeDtypeStruct((SHARD, WIDTH), F32),
            jax.ShapeDtypeStruct((ROWS,), F32),
        ),
        in_specs=[anywhere] * 4,
        out_specs=(vmem, vmem),
        scratch_shapes=[
            pltpu.SMEM((LISTED, CLUSTERS), jnp.int32),
            pltpu.VMEM((ROWS, WIDTH), BF16),
            pltpu.VMEM((1, ROWS), jnp.int32),
            pltpu.VMEM((GROUPS, SLOTS, WIDTH), BF16),
            pltpu.VMEM((GROUPS, SLOTS, WIDTH), BF16),
            pltpu.VMEM((GROUPS, 8, SLOTS), F32),
            pltpu.VMEM((GROUPS, 8, SLOTS), F32),
            pltpu.VMEM((MEMBERS, SHARD, WIDTH), BF16),
            pltpu.VMEM((8, BLK, SLOTS), F32),
            pltpu.VMEM((4, 4 * SHARD, 2 * SLOTS), F32),
            pltpu.VMEM((MEMBERS, SHARD, GROUPS * SLOTS), BF16),
            pltpu.VMEM((GROUPS, 8, SLOTS), F32),
            pltpu.VMEM((GROUPS, 8, SLOTS), F32),
            pltpu.VMEM((4, 4, 8, BLK), F32),
            pltpu.VMEM((4, 4, 8, BLK), F32),
            pltpu.VMEM((4, 8, BLK), F32),
            pltpu.VMEM((4, 8, BLK), F32),
            pltpu.VMEM((4, 4, SHARD, HALF), BF16),
            pltpu.VMEM((4, 4, SHARD, HALF), BF16),
            pltpu.VMEM((4, 4, SHARD, HALF), F32),
            pltpu.VMEM((4, 4, SHARD, HALF), F32),
            pltpu.VMEM((MEMBERS, SHARD, BLK), F32),
            pltpu.VMEM((4, SHARD, HALF), F32),
            pltpu.VMEM((4, SHARD, HALF), F32),
            pltpu.VMEM((2, 4, SHARD, QUARTER), BF16),
            pltpu.VMEM((2, 4, SHARD, QUARTER), BF16),
            pltpu.VMEM((2, 4, SHARD, HALF), BF16),
            pltpu.VMEM((2, 4, SHARD, HALF), BF16),
            pltpu.VMEM((4, SHARD, HALF), BF16),
            pltpu.VMEM((4, SHARD, HALF), BF16),
            pltpu.VMEM((3, SHARD, HALF), BF16),
            pltpu.VMEM((3, SHARD, HALF), BF16),
            dma((4,)),
            dma,
            dma((len(BATCHES) + 1,)),
            dma((2,)),
            dma((2,)),
            dma((4,)),
            dma,
            dma((2, 3)),
            dma,
            dma((2,)),
            dma((2, SUBS)),
            dma((2, SUBS)),
            dma((2,)),
            dma((2,)),
        ],
        compiler_params=pltpu.CompilerParams(
            collective_id=0, has_side_effects=True, vmem_limit_bytes=32 << 20
        ),
    )(*(pltpu.with_memory_space_constraint(a, pltpu.HBM) for a in operands))
    return updated, affinity


def solution(mesh):
    return jax.shard_map(
        local,
        mesh=mesh,
        in_specs=(P(("grp", "dev"), None), P(("grp", "dev"), None), P(), P(("grp", "dev"), None)),
        out_specs=(P(("grp", "dev"), None), P(("grp", "dev"))),
        check_vma=False,
    )
```

```python
import jax
import jax.numpy as jnp
from jax import lax
from jax.experimental import pallas as pl
from jax.experimental.pallas import tpu as pltpu
from jax.sharding import PartitionSpec as P

MESH = pl.DeviceIdType.MESH
F32 = jnp.float32
BF16 = jnp.bfloat16

SOFTMAX_TEMP = 0.4
PRIOR_WEIGHT = 1.0
FAR = 1e30

GROUPS = 8
MEMBERS = 16
ROWS = 512
WIDTH = 1024
SHARD = 64
POOL = MEMBERS * SHARD
PER_GROUP = 4
CLUSTERS = 32
CAP = 32
LISTED = 4
BLK = 128
SLOTS = PER_GROUP * CAP
HALF = WIDTH // 2
QUARTER = WIDTH // 4
SPANS = ((0, 1), (1, 2), (2, 4))
SUBS = len(SPANS)
EARLY = 6
AWAY = ((0, 0), (0, 1), (1, 0), (3, 0), (1, 1), (3, 1), (2, 0), (2, 1))
ORDER = ((2, 3), (4, 5), (6, 7), (1, 0))
BATCHES = ((0, 1), (2, 3), (4, 5), (6,), (7,))
LAST = GROUPS - 1


def iota(shape, axis):
    return lax.broadcasted_iota(jnp.int32, shape, axis)


def kernel(
    cand_hbm,
    points_hbm,
    coarse_hbm,
    cent_hbm,
    new_ref,
    aff_ref,
    cand,
    points,
    coarse,
    tx,
    rx,
    txf,
    rxf,
    pool,
    norms,
    logits,
    weights,
    afftx,
    affrx,
    tot1,
    tot1rx,
    tot2,
    tot2rx,
    part_a,
    part_b,
    acc_a,
    acc_b,
    early,
    own_a,
    own_b,
    far_a,
    far_b,
    near_a,
    near_b,
    send_a,
    send_b,
    last_a,
    last_b,
    in_sem,
    row_send,
    row_recv,
    flag_sem,
    aff_sem,
    tot_sem,
    ag_send,
    ag1_recv,
    ag2_recv,
    part_send,
    far_recv,
    near_recv,
    last_send,
    last_recv,
):
    g = lax.axis_index("grp")
    d = lax.axis_index("dev")
    x, c = lax.div(g, 2), lax.rem(g, 2)
    z, y = lax.div(d, 4), lax.rem(d, 4)

    def group_at(k):
        return lax.rem(x + AWAY[k][0], 4) * 2 + lax.rem(c + AWAY[k][1], 2)

    def group_from(k):
        return lax.rem(x + 4 - AWAY[k][0], 4) * 2 + lax.rem(c + AWAY[k][1], 2)

    def turn(value, by):
        return lax.rem(value + by + 4, 4)

    def member(first, second, axis):
        return first * 4 + second if axis == 0 else second * 4 + first

    place = ((z, y), (y, z))

    def remote(src, dst, send_sem, recv_sem, device):
        return pltpu.make_async_remote_copy(
            src_ref=src,
            dst_ref=dst,
            send_sem=send_sem,
            recv_sem=recv_sem,
            device_id=device,
            device_id_type=MESH,
        )

    coarse_in = pltpu.make_async_copy(coarse_hbm, coarse, in_sem.at[0])
    points_in = pltpu.make_async_copy(points_hbm, points, in_sem.at[1])
    coarse_in.start()
    points_in.start()

    barrier = pltpu.get_barrier_semaphore()
    for k in range(1, GROUPS):
        pl.semaphore_signal(barrier, inc=1, device_id=(group_at(k), d), device_id_type=MESH)
    for axis in (0, 1):
        first, second = place[axis]
        for k in range(1, 4):
            pl.semaphore_signal(
                barrier,
                inc=1,
                device_id=(g, member(turn(first, k), second, axis)),
                device_id_type=MESH,
            )

    cent_in = pltpu.make_async_copy(cent_hbm, pool.at[d], in_sem.at[2])
    cand_in = pltpu.make_async_copy(cand_hbm, cand, in_sem.at[3])
    cent_in.start()
    cand_in.start()

    cluster_ids = iota((CLUSTERS, ROWS), 0)
    before = (iota((ROWS, ROWS), 0) < iota((ROWS, ROWS), 1)).astype(F32).astype(BF16)
    coarse_in.wait()
    named = (coarse[...] == cluster_ids).astype(F32)
    rank = jnp.dot(named.astype(BF16), before, preferred_element_type=F32)
    slot = jnp.sum(named * (rank + (cluster_ids * CAP).astype(F32)), axis=0, keepdims=True)
    count = jnp.sum(named, axis=1, keepdims=True)
    slot_ids = iota((SLOTS, ROWS), 0)
    lane = iota((CLUSTERS, SLOTS), 1)
    lane_cluster, lane_rank = lax.div(lane, CAP), lax.rem(lane, CAP)

    def flag(owner):
        mine = iota((CLUSTERS, SLOTS), 0) == lane_cluster + owner * PER_GROUP
        held = jnp.sum(jnp.where(mine, count, 0.0), axis=0, keepdims=True)
        live = (lane_rank[0:1].astype(F32) < held).astype(F32)
        return jnp.broadcast_to(live, (8, SLOTS))

    def pack(pair):
        here = jnp.concatenate(
            [slot == (slot_ids + group_at(k) * SLOTS).astype(F32) for k in pair], axis=0
        )
        rows = jnp.dot(here.astype(F32).astype(BF16), points[...], preferred_element_type=F32)
        for i, k in enumerate(pair):
            (tx if k else rx)[k] = rows[i * SLOTS : (i + 1) * SLOTS].astype(BF16)

    def columns(axis):
        return pl.ds(axis * HALF, HALF)

    def row_copy(k):
        number = [k in batch for batch in BATCHES].index(True)
        return remote(tx.at[k], rx.at[k], row_send, row_recv.at[number], (group_at(k), d))

    def last_row_copy(half):
        span = columns(half)
        return remote(
            tx.at[LAST, :, span],
            rx.at[LAST, :, span],
            row_send,
            row_recv.at[len(BATCHES) - 1 + half],
            (group_at(LAST), d),
        )

    def flag_copy(k):
        return remote(txf.at[k], rxf.at[k], flag_sem.at[0], flag_sem.at[1], (group_at(k), d))

    def aff_copy(k):
        return remote(afftx.at[k], affrx.at[k], aff_sem.at[0], aff_sem.at[1], (group_from(k), d))

    def arrived(ref, sem):
        remote(ref, ref, sem, sem, (g, d)).wait_recv()

    def left(ref, sem):
        remote(ref, ref, sem, sem, (g, d)).wait_send()

    def gather1(axis, k):
        first, second = place[axis]
        piece = pool.at[d, :, columns(axis)]
        return remote(
            piece,
            piece,
            ag_send,
            ag1_recv.at[axis, k - 1],
            (g, member(turn(first, k), second, axis)),
        )

    def gather2(axis, k1, k2):
        first, second = place[axis]
        piece = pool.at[member(turn(first, -k1), second, axis), :, columns(axis)]
        return remote(
            piece,
            piece,
            ag_send,
            ag2_recv,
            (g, member(first, turn(second, k2), axis)),
        )

    for k in range(1, GROUPS):
        txf[k] = flag(group_at(k))
    rxf[0] = flag(g)
    points_in.wait()
    pack(ORDER[0])
    pl.semaphore_wait(barrier, GROUPS - 1 + 6)
    for i, pair in enumerate(ORDER):
        if i:
            pack(pair)
        for k in pair:
            if k == LAST:
                last_row_copy(0).start()
                last_row_copy(1).start()
            elif k:
                row_copy(k).start()
        if i == 0:
            for k in range(1, GROUPS):
                flag_copy(k).start()
            cent_in.wait()
            for axis in (0, 1):
                for k1 in (2, 1, 3):
                    gather1(axis, k1).start()
        if i == 1:
            for axis in (0, 1):
                for k2 in (2, 1, 3):
                    gather2(axis, 0, k2).start()

    for k1 in (1, 3, 2):
        for axis in (0, 1):
            gather1(axis, k1).wait_recv()
            for k2 in (2, 1, 3):
                gather2(axis, k1, k2).start()

    cand_in.wait()
    block = iota((8, SLOTS), 0)
    allowed = jnp.zeros((8, SLOTS), jnp.bool_)
    wide_cluster = lax.div(iota((8, SLOTS), 1), CAP)
    for cluster in range(PER_GROUP):
        for j in range(LISTED):
            listed = cand[j, g * PER_GROUP + cluster]
            allowed = allowed | ((block == listed) & (wide_cluster == cluster))
    penalty = jnp.where(allowed, 0.0, FAR)

    arrived(pool.at[0:12], ag2_recv)
    arrived(rxf.at[1:GROUPS], flag_sem.at[1])

    for b in range(8):
        rows = pool[2 * b : 2 * b + 2].reshape(BLK, WIDTH).astype(F32)
        square = jnp.sum(rows * rows, axis=1, keepdims=True)
        norms[b] = square + penalty[b : b + 1]

    def score(number, pair):
        if pair[0] == LAST:
            arrived(rx.at[LAST, :, columns(0)], row_recv.at[number])
        else:
            first = max(pair[0], 1)
            arrived(rx.at[first : pair[-1] + 1], row_recv.at[number])
        live = jnp.concatenate([rxf[k, 0:1] for k in pair], axis=1)

        wide = len(pair) * SLOTS

        def inner_products(t, span):
            return lax.dot_general(
                pool[4 * t : 4 * t + 4, :, span].reshape(4 * SHARD, -1),
                rx[pair[0] : pair[-1] + 1, :, span].reshape(wide, -1),
                (((1,), (1,)), ((), ())),
                preferred_element_type=F32,
            )

        if pair[0] == LAST:
            for t in range(4):
                logits[t, :, :wide] = inner_products(t, slice(0, HALF))
            arrived(rx.at[LAST, :, columns(1)], row_recv.at[number + 1])
        top = jnp.full((1, wide), -jnp.inf, F32)
        for t in range(4):
            if pair[0] == LAST:
                inner = logits[t, :, :wide] + inner_products(t, slice(HALF, WIDTH))
            else:
                inner = inner_products(t, slice(0, WIDTH))
            square = norms[2 * t : 2 * t + 2].reshape(4 * SHARD, SLOTS)
            square = jnp.concatenate([square] * len(pair), axis=1)
            value = (2.0 * inner - square) * (1.0 / SOFTMAX_TEMP)
            logits[t, :, :wide] = value
            top = jnp.maximum(top, jnp.max(value, axis=0, keepdims=True))
        total = jnp.zeros((1, wide), F32)
        for t in range(4):
            value = jnp.exp(logits[t, :, :wide] - top)
            logits[t, :, :wide] = value
            total = total + jnp.sum(value, axis=0, keepdims=True)
        scale = live / total
        for t in range(4):
            value = (logits[t, :, :wide] * scale).astype(BF16).reshape(4, SHARD, wide)
            weights[4 * t : 4 * t + 4, :, pair[0] * SLOTS : (pair[-1] + 1) * SLOTS] = value
        affinity = SOFTMAX_TEMP * (top + jnp.log(total))
        for i, k in enumerate(pair):
            mine = jnp.broadcast_to(affinity[:, i * SLOTS : (i + 1) * SLOTS], (8, SLOTS))
            if k:
                afftx[k] = mine
                aff_copy(k).start()
            else:
                affrx[0] = mine

    acc = (acc_a, acc_b)

    def partial(axis, index, low, high):
        lanes = slice(low * SLOTS, high * SLOTS)
        lhs = jnp.concatenate([weights[member(index, i, axis), :, lanes] for i in range(4)], axis=0)
        rhs = rx[low:high, :, axis * HALF : (axis + 1) * HALF].reshape((high - low) * SLOTS, HALF)
        return jnp.dot(lhs, rhs, preferred_element_type=F32).reshape(4, SHARD, HALF)

    def product(axis, index):
        return acc[axis][index] + partial(axis, index, EARLY, GROUPS)

    def lane_sums(i, low, high):
        total = weights[i, :, low * SLOTS : (low + 1) * SLOTS].astype(F32)
        for k in range(low + 1, high):
            total = total + weights[i, :, k * SLOTS : (k + 1) * SLOTS].astype(F32)
        return total

    def early_sums(i, carry):
        early[i] = lane_sums(i, 0, EARLY)
        return carry

    for number, pair in enumerate(BATCHES):
        if pair[0] == EARLY:
            for axis in (0, 1):
                for index in range(4):
                    acc[axis][index] = partial(axis, index, 0, EARLY)
            lax.fori_loop(0, MEMBERS, early_sums, 0)
        score(number, pair)

    part = (part_a, part_b)
    own = (own_a, own_b)
    far_in, near_in = (far_a, far_b), (near_a, near_b)
    send, last = (send_a, send_b), (last_a, last_b)

    def span_of(sub):
        return pl.ds(SPANS[sub][0], SPANS[sub][1] - SPANS[sub][0])

    def hop(axis, sub, side, near, piece):
        first, second = place[axis]
        step = 1 - 2 * side
        span = pl.ds(piece * QUARTER, QUARTER)
        source = part[axis].at[turn(first, step if near else 2), span_of(sub), :, span]
        target = (g, member(turn(first, step), second, axis))
        if near:
            landing = near_in[axis].at[side, span_of(sub), :, span]
            return remote(source, landing, part_send.at[axis], near_recv.at[axis, sub], target)
        landing = far_in[axis].at[side, span_of(sub)]
        return remote(source, landing, part_send.at[axis], far_recv.at[axis, sub], target)

    def far(axis, sub):
        for side in (0, 1):
            hop(axis, sub, side, False, side).start()

    def direct(axis, sub):
        for side in (0, 1):
            hop(axis, sub, side, True, 1 - side).start()

    def relay(axis, sub):
        low, high = SPANS[sub]
        arrived(far_in[axis].at[:, span_of(sub)], far_recv.at[axis, sub])
        for side in (0, 1):
            index = turn(place[axis][0], 1 - 2 * side)
            span = slice(side * QUARTER, (side + 1) * QUARTER)
            part[axis][index, low:high, :, span] = (
                part[axis][index, low:high, :, span].astype(F32)
                + far_in[axis][side, low:high].astype(F32)
            ).astype(BF16)
            hop(axis, sub, side, True, side).start()

    def final(axis, sub):
        first, second = place[axis]
        low, high = SPANS[sub]
        arrived(near_in[axis].at[:, span_of(sub)], near_recv.at[axis, sub])
        total = own[axis][low:high]
        for side in (0, 1):
            total = total + near_in[axis][side, low:high].astype(F32)
        own[axis][low:high] = total
        send[axis][low:high] = total.astype(BF16)
        for holder in range(low, high):

            @pl.when(second != holder)
            def _():
                remote(
                    send[axis].at[holder],
                    last[axis].at[turn(second, -holder) - 1],
                    last_send.at[axis],
                    last_recv.at[axis],
                    (g, member(first, holder, axis)),
                ).start()

    for axis in (0, 1):
        index = turn(place[axis][0], 2)
        part[axis][index] = product(axis, index).astype(BF16)
        for sub in range(SUBS):
            far(axis, sub)
    for axis in (0, 1):
        for side in (0, 1):
            index = turn(place[axis][0], 1 - 2 * side)
            part[axis][index] = product(axis, index).astype(BF16)
        for sub in range(SUBS):
            direct(axis, sub)
    for axis in (0, 1):
        own[axis][...] = product(axis, place[axis][0])

    lanes = iota((SHARD, BLK), 1)
    diagonal = lanes == iota((SHARD, BLK), 0)

    def total1(k):
        to = turn(z, k)
        return remote(tot1.at[to], tot1rx.at[k], tot_sem.at[0], tot_sem.at[1], (g, to * 4 + y))

    def total2(k):
        to = turn(y, k)
        return remote(tot2.at[to], tot2rx.at[k], tot_sem.at[2], tot_sem.at[3], (g, z * 4 + to))

    def total_of(i, carry):
        for j in range(4):
            found = early[4 * i + j] + lane_sums(4 * i + j, EARLY, GROUPS)
            column = jnp.sum(found, axis=1, keepdims=True)
            row = jnp.sum(jnp.where(diagonal, column, 0.0), axis=0, keepdims=True)
            tot1[i, j] = jnp.broadcast_to(row, (8, BLK))
        return carry

    lax.fori_loop(0, 4, total_of, 0)

    for axis in (0, 1):
        relay(axis, 0)
    for axis in (0, 1):
        relay(axis, 1)
    for k in range(1, 4):
        total1(k).start()
    for axis in (0, 1):
        relay(axis, 2)
    for axis in (0, 1):
        final(axis, 0)
    arrived(tot1rx.at[1:4], tot_sem.at[1])
    totals = tot1[z]
    for k in range(1, 4):
        totals = totals + tot1rx[k]
    tot2[...] = totals
    for k in range(1, 4):
        total2(k).start()
    for axis in (0, 1):
        final(axis, 1)
    for axis in (0, 1):
        final(axis, 2)

    affinity = jnp.zeros((1, ROWS), F32)
    square_eye = iota((SLOTS, SLOTS), 0) == iota((SLOTS, SLOTS), 1)
    arrived(affrx.at[1:GROUPS], aff_sem.at[1])
    for k in range(GROUPS):
        column = jnp.sum(jnp.where(square_eye, affrx[k, 0:1], 0.0), axis=1, keepdims=True)
        here = slot == (slot_ids + group_at(k) * SLOTS).astype(F32)
        affinity = affinity + jnp.sum(jnp.where(here, column, 0.0), axis=0, keepdims=True)
    aff_ref[...] = affinity.reshape(ROWS)

    totals = tot2[y]
    arrived(tot2rx.at[1:4], tot_sem.at[3])
    for k in range(1, 4):
        totals = totals + tot2rx[k]
    column = jnp.sum(jnp.where(diagonal, totals[0:1], 0.0), axis=1, keepdims=True) + PRIOR_WEIGHT
    scale = 1.0 / column

    for axis in (0, 1):
        second = place[axis][1]
        span = slice(axis * HALF, (axis + 1) * HALF)
        total = own[axis][second] + PRIOR_WEIGHT * pool[d, :, span].astype(F32)
        arrived(last[axis], last_recv.at[axis])
        for k in range(3):
            total = total + last[axis][k].astype(F32)
        new_ref[:, span] = total * scale

    left(tx.at[1:GROUPS], row_send)
    left(txf.at[1:GROUPS], flag_sem.at[0])
    left(afftx.at[1:GROUPS], aff_sem.at[0])
    left(tot1.at[0:3], tot_sem.at[0])
    left(tot2.at[0:3], tot_sem.at[2])
    left(pool.at[0:15], ag_send)
    for axis in (0, 1):
        left(part[axis].at[0:3], part_send.at[axis])
        left(last[axis], last_send.at[axis])


def local(points, coarse, candidates, centroids):
    operands = (candidates.T, points, coarse.reshape(1, ROWS), centroids)
    vmem = pl.BlockSpec(memory_space=pltpu.VMEM)
    anywhere = pl.BlockSpec(memory_space=pl.ANY)
    dma = pltpu.SemaphoreType.DMA
    updated, affinity = pl.pallas_call(
        kernel,
        out_shape=(
            jax.ShapeDtypeStruct((SHARD, WIDTH), F32),
            jax.ShapeDtypeStruct((ROWS,), F32),
        ),
        in_specs=[anywhere] * 4,
        out_specs=(vmem, vmem),
        scratch_shapes=[
            pltpu.SMEM((LISTED, CLUSTERS), jnp.int32),
            pltpu.VMEM((ROWS, WIDTH), BF16),
            pltpu.VMEM((1, ROWS), jnp.int32),
            pltpu.VMEM((GROUPS, SLOTS, WIDTH), BF16),
            pltpu.VMEM((GROUPS, SLOTS, WIDTH), BF16),
            pltpu.VMEM((GROUPS, 8, SLOTS), F32),
            pltpu.VMEM((GROUPS, 8, SLOTS), F32),
            pltpu.VMEM((MEMBERS, SHARD, WIDTH), BF16),
            pltpu.VMEM((8, BLK, SLOTS), F32),
            pltpu.VMEM((4, 4 * SHARD, 2 * SLOTS), F32),
            pltpu.VMEM((MEMBERS, SHARD, GROUPS * SLOTS), BF16),
            pltpu.VMEM((GROUPS, 8, SLOTS), F32),
            pltpu.VMEM((GROUPS, 8, SLOTS), F32),
            pltpu.VMEM((4, 4, 8, BLK), F32),
            pltpu.VMEM((4, 4, 8, BLK), F32),
            pltpu.VMEM((4, 8, BLK), F32),
            pltpu.VMEM((4, 8, BLK), F32),
            pltpu.VMEM((4, 4, SHARD, HALF), BF16),
            pltpu.VMEM((4, 4, SHARD, HALF), BF16),
            pltpu.VMEM((4, 4, SHARD, HALF), F32),
            pltpu.VMEM((4, 4, SHARD, HALF), F32),
            pltpu.VMEM((MEMBERS, SHARD, BLK), F32),
            pltpu.VMEM((4, SHARD, HALF), F32),
            pltpu.VMEM((4, SHARD, HALF), F32),
            pltpu.VMEM((2, 4, SHARD, QUARTER), BF16),
            pltpu.VMEM((2, 4, SHARD, QUARTER), BF16),
            pltpu.VMEM((2, 4, SHARD, HALF), BF16),
            pltpu.VMEM((2, 4, SHARD, HALF), BF16),
            pltpu.VMEM((4, SHARD, HALF), BF16),
            pltpu.VMEM((4, SHARD, HALF), BF16),
            pltpu.VMEM((3, SHARD, HALF), BF16),
            pltpu.VMEM((3, SHARD, HALF), BF16),
            dma((4,)),
            dma,
            dma((len(BATCHES) + 1,)),
            dma((2,)),
            dma((2,)),
            dma((4,)),
            dma,
            dma((2, 3)),
            dma,
            dma((2,)),
            dma((2, SUBS)),
            dma((2, SUBS)),
            dma((2,)),
            dma((2,)),
        ],
        compiler_params=pltpu.CompilerParams(
            collective_id=0, has_side_effects=True, vmem_limit_bytes=32 << 20
        ),
    )(*(pltpu.with_memory_space_constraint(a, pltpu.HBM) for a in operands))
    return updated, affinity


def solution(mesh):
    return jax.shard_map(
        local,
        mesh=mesh,
        in_specs=(P(("grp", "dev"), None), P(("grp", "dev"), None), P(), P(("grp", "dev"), None)),
        out_specs=(P(("grp", "dev"), None), P(("grp", "dev"))),
        check_vma=False,
    )
```

```python
import jax
import jax.numpy as jnp
from jax import lax
from jax.experimental import pallas as pl
from jax.experimental.pallas import tpu as pltpu
from jax.sharding import PartitionSpec as P

MESH = pl.DeviceIdType.MESH
F32 = jnp.float32
BF16 = jnp.bfloat16

SOFTMAX_TEMP = 0.4
PRIOR_WEIGHT = 1.0
FAR = 1e30

GROUPS = 8
MEMBERS = 16
ROWS = 512
WIDTH = 1024
SHARD = 64
POOL = MEMBERS * SHARD
PER_GROUP = 4
CLUSTERS = 32
CAP = 32
LISTED = 4
BLK = 128
SLOTS = PER_GROUP * CAP
HALF = WIDTH // 2
QUARTER = WIDTH // 4
SPANS = ((0, 1), (1, 2), (2, 4))
SUBS = len(SPANS)
EARLY = 6
AWAY = ((0, 0), (0, 1), (1, 0), (3, 0), (1, 1), (3, 1), (2, 0), (2, 1))
ORDER = (2, 3, 4, 5, 6, 7, 1)
BATCHES = ((0, 1), (2, 3), (4, 5), (6,), (7,))
LAST = GROUPS - 1


def iota(shape, axis):
    return lax.broadcasted_iota(jnp.int32, shape, axis)


def kernel(
    cand_hbm,
    points_hbm,
    coarse_hbm,
    cent_hbm,
    new_ref,
    aff_ref,
    cand,
    points,
    coarse,
    tx,
    rx,
    txf,
    rxf,
    pool,
    norms,
    logits,
    weights,
    afftx,
    affrx,
    tot1,
    tot1rx,
    tot2,
    tot2rx,
    part_a,
    part_b,
    acc_a,
    acc_b,
    early,
    own_a,
    own_b,
    far_a,
    far_b,
    near_a,
    near_b,
    send_a,
    send_b,
    last_a,
    last_b,
    in_sem,
    row_send,
    row_recv,
    flag_sem,
    aff_sem,
    tot_sem,
    ag_send,
    ag1_recv,
    ag2_recv,
    part_send,
    far_recv,
    near_recv,
    last_send,
    last_recv,
):
    g = lax.axis_index("grp")
    d = lax.axis_index("dev")
    x, c = lax.div(g, 2), lax.rem(g, 2)
    z, y = lax.div(d, 4), lax.rem(d, 4)

    def group_at(k):
        return lax.rem(x + AWAY[k][0], 4) * 2 + lax.rem(c + AWAY[k][1], 2)

    def group_from(k):
        return lax.rem(x + 4 - AWAY[k][0], 4) * 2 + lax.rem(c + AWAY[k][1], 2)

    def turn(value, by):
        return lax.rem(value + by + 4, 4)

    def member(first, second, axis):
        return first * 4 + second if axis == 0 else second * 4 + first

    place = ((z, y), (y, z))

    def remote(src, dst, send_sem, recv_sem, device):
        return pltpu.make_async_remote_copy(
            src_ref=src,
            dst_ref=dst,
            send_sem=send_sem,
            recv_sem=recv_sem,
            device_id=device,
            device_id_type=MESH,
        )

    coarse_in = pltpu.make_async_copy(coarse_hbm, coarse, in_sem.at[0])
    points_in = pltpu.make_async_copy(points_hbm, points, in_sem.at[1])
    coarse_in.start()
    points_in.start()

    barrier = pltpu.get_barrier_semaphore()
    for k in range(1, GROUPS):
        pl.semaphore_signal(barrier, inc=1, device_id=(group_at(k), d), device_id_type=MESH)
    for axis in (0, 1):
        first, second = place[axis]
        for k in range(1, 4):
            pl.semaphore_signal(
                barrier,
                inc=1,
                device_id=(g, member(turn(first, k), second, axis)),
                device_id_type=MESH,
            )

    cent_in = pltpu.make_async_copy(cent_hbm, pool.at[d], in_sem.at[2])
    cand_in = pltpu.make_async_copy(cand_hbm, cand, in_sem.at[3])
    cent_in.start()
    cand_in.start()

    cluster_ids = iota((CLUSTERS, ROWS), 0)
    before = (iota((ROWS, ROWS), 0) < iota((ROWS, ROWS), 1)).astype(F32).astype(BF16)
    coarse_in.wait()
    named = (coarse[...] == cluster_ids).astype(F32)
    rank = jnp.dot(named.astype(BF16), before, preferred_element_type=F32)
    slot = jnp.sum(named * (rank + (cluster_ids * CAP).astype(F32)), axis=0, keepdims=True)
    count = jnp.sum(named, axis=1, keepdims=True)
    slot_ids = iota((SLOTS, ROWS), 0)
    lane = iota((CLUSTERS, SLOTS), 1)
    lane_cluster, lane_rank = lax.div(lane, CAP), lax.rem(lane, CAP)

    def flag(owner):
        mine = iota((CLUSTERS, SLOTS), 0) == lane_cluster + owner * PER_GROUP
        held = jnp.sum(jnp.where(mine, count, 0.0), axis=0, keepdims=True)
        live = (lane_rank[0:1].astype(F32) < held).astype(F32)
        return jnp.broadcast_to(live, (8, SLOTS))

    def pack(owner):
        here = slot == (slot_ids + owner * SLOTS).astype(F32)
        return jnp.dot(
            here.astype(F32).astype(BF16), points[...], preferred_element_type=F32
        ).astype(BF16)

    def columns(axis):
        return pl.ds(axis * HALF, HALF)

    def row_copy(k):
        number = [k in batch for batch in BATCHES].index(True)
        return remote(tx.at[k], rx.at[k], row_send, row_recv.at[number], (group_at(k), d))

    def last_row_copy(half):
        span = columns(half)
        return remote(
            tx.at[LAST, :, span],
            rx.at[LAST, :, span],
            row_send,
            row_recv.at[len(BATCHES) - 1 + half],
            (group_at(LAST), d),
        )

    def flag_copy(k):
        return remote(txf.at[k], rxf.at[k], flag_sem.at[0], flag_sem.at[1], (group_at(k), d))

    def aff_copy(k):
        return remote(afftx.at[k], affrx.at[k], aff_sem.at[0], aff_sem.at[1], (group_from(k), d))

    def arrived(ref, sem):
        remote(ref, ref, sem, sem, (g, d)).wait_recv()

    def left(ref, sem):
        remote(ref, ref, sem, sem, (g, d)).wait_send()

    def gather1(axis, k):
        first, second = place[axis]
        piece = pool.at[d, :, columns(axis)]
        return remote(
            piece,
            piece,
            ag_send,
            ag1_recv.at[axis, k - 1],
            (g, member(turn(first, k), second, axis)),
        )

    def gather2(axis, k1, k2):
        first, second = place[axis]
        piece = pool.at[member(turn(first, -k1), second, axis), :, columns(axis)]
        return remote(
            piece,
            piece,
            ag_send,
            ag2_recv,
            (g, member(first, turn(second, k2), axis)),
        )

    for k in ORDER:
        txf[k] = flag(group_at(k))
    rxf[0] = flag(g)
    points_in.wait()
    tx[ORDER[0]] = pack(group_at(ORDER[0]))
    pl.semaphore_wait(barrier, GROUPS - 1 + 6)
    for i, k in enumerate(ORDER):
        if i:
            tx[k] = pack(group_at(k))
        if k == LAST:
            last_row_copy(0).start()
            last_row_copy(1).start()
        else:
            row_copy(k).start()
        if i == 1:
            for k1 in ORDER:
                flag_copy(k1).start()
            cent_in.wait()
            for axis in (0, 1):
                for k1 in (2, 1, 3):
                    gather1(axis, k1).start()
        if i == 2:
            for axis in (0, 1):
                for k2 in (2, 1, 3):
                    gather2(axis, 0, k2).start()
    rx[0] = pack(g)

    for k1 in (1, 3, 2):
        for axis in (0, 1):
            gather1(axis, k1).wait_recv()
            for k2 in (2, 1, 3):
                gather2(axis, k1, k2).start()

    cand_in.wait()
    block = iota((8, SLOTS), 0)
    allowed = jnp.zeros((8, SLOTS), jnp.bool_)
    wide_cluster = lax.div(iota((8, SLOTS), 1), CAP)
    for cluster in range(PER_GROUP):
        for j in range(LISTED):
            listed = cand[j, g * PER_GROUP + cluster]
            allowed = allowed | ((block == listed) & (wide_cluster == cluster))
    penalty = jnp.where(allowed, 0.0, FAR)

    arrived(pool.at[0:12], ag2_recv)
    arrived(rxf.at[1:GROUPS], flag_sem.at[1])

    for b in range(8):
        rows = pool[2 * b : 2 * b + 2].reshape(BLK, WIDTH).astype(F32)
        square = jnp.sum(rows * rows, axis=1, keepdims=True)
        norms[b] = square + penalty[b : b + 1]

    def score(number, pair):
        if pair[0] == LAST:
            arrived(rx.at[LAST, :, columns(0)], row_recv.at[number])
        else:
            first = max(pair[0], 1)
            arrived(rx.at[first : pair[-1] + 1], row_recv.at[number])
        live = jnp.concatenate([rxf[k, 0:1] for k in pair], axis=1)

        wide = len(pair) * SLOTS

        def inner_products(t, span):
            return lax.dot_general(
                pool[4 * t : 4 * t + 4, :, span].reshape(4 * SHARD, -1),
                rx[pair[0] : pair[-1] + 1, :, span].reshape(wide, -1),
                (((1,), (1,)), ((), ())),
                preferred_element_type=F32,
            )

        if pair[0] == LAST:
            for t in range(4):
                logits[t, :, :wide] = inner_products(t, slice(0, HALF))
            arrived(rx.at[LAST, :, columns(1)], row_recv.at[number + 1])
        top = jnp.full((1, wide), -jnp.inf, F32)
        for t in range(4):
            if pair[0] == LAST:
                inner = logits[t, :, :wide] + inner_products(t, slice(HALF, WIDTH))
            else:
                inner = inner_products(t, slice(0, WIDTH))
            square = norms[2 * t : 2 * t + 2].reshape(4 * SHARD, SLOTS)
            square = jnp.concatenate([square] * len(pair), axis=1)
            value = (2.0 * inner - square) * (1.0 / SOFTMAX_TEMP)
            logits[t, :, :wide] = value
            top = jnp.maximum(top, jnp.max(value, axis=0, keepdims=True))
        total = jnp.zeros((1, wide), F32)
        for t in range(4):
            value = jnp.exp(logits[t, :, :wide] - top)
            logits[t, :, :wide] = value
            total = total + jnp.sum(value, axis=0, keepdims=True)
        scale = live / total
        for t in range(4):
            value = (logits[t, :, :wide] * scale).astype(BF16).reshape(4, SHARD, wide)
            weights[4 * t : 4 * t + 4, :, pair[0] * SLOTS : (pair[-1] + 1) * SLOTS] = value
        affinity = SOFTMAX_TEMP * (top + jnp.log(total))
        for i, k in enumerate(pair):
            mine = jnp.broadcast_to(affinity[:, i * SLOTS : (i + 1) * SLOTS], (8, SLOTS))
            if k:
                afftx[k] = mine
                aff_copy(k).start()
            else:
                affrx[0] = mine

    acc = (acc_a, acc_b)

    def partial(axis, index, low, high):
        lanes = slice(low * SLOTS, high * SLOTS)
        lhs = jnp.concatenate([weights[member(index, i, axis), :, lanes] for i in range(4)], axis=0)
        rhs = rx[low:high, :, axis * HALF : (axis + 1) * HALF].reshape((high - low) * SLOTS, HALF)
        return jnp.dot(lhs, rhs, preferred_element_type=F32).reshape(4, SHARD, HALF)

    def product(axis, index):
        return acc[axis][index] + partial(axis, index, EARLY, GROUPS)

    def lane_sums(i, low, high):
        total = weights[i, :, low * SLOTS : (low + 1) * SLOTS].astype(F32)
        for k in range(low + 1, high):
            total = total + weights[i, :, k * SLOTS : (k + 1) * SLOTS].astype(F32)
        return total

    def early_sums(i, carry):
        early[i] = lane_sums(i, 0, EARLY)
        return carry

    for number, pair in enumerate(BATCHES):
        if pair[0] == EARLY:
            for axis in (0, 1):
                for index in range(4):
                    acc[axis][index] = partial(axis, index, 0, EARLY)
            lax.fori_loop(0, MEMBERS, early_sums, 0)
        score(number, pair)

    part = (part_a, part_b)
    own = (own_a, own_b)
    far_in, near_in = (far_a, far_b), (near_a, near_b)
    send, last = (send_a, send_b), (last_a, last_b)

    def span_of(sub):
        return pl.ds(SPANS[sub][0], SPANS[sub][1] - SPANS[sub][0])

    def hop(axis, sub, side, near, piece):
        first, second = place[axis]
        step = 1 - 2 * side
        span = pl.ds(piece * QUARTER, QUARTER)
        source = part[axis].at[turn(first, step if near else 2), span_of(sub), :, span]
        target = (g, member(turn(first, step), second, axis))
        if near:
            landing = near_in[axis].at[side, span_of(sub), :, span]
            return remote(source, landing, part_send, near_recv.at[axis, sub], target)
        landing = far_in[axis].at[side, span_of(sub)]
        return remote(source, landing, part_send, far_recv.at[axis, sub], target)

    def far(axis, sub):
        for side in (0, 1):
            hop(axis, sub, side, False, side).start()

    def direct(axis, sub):
        for side in (0, 1):
            hop(axis, sub, side, True, 1 - side).start()

    def relay(axis, sub):
        low, high = SPANS[sub]
        arrived(far_in[axis].at[:, span_of(sub)], far_recv.at[axis, sub])
        for side in (0, 1):
            index = turn(place[axis][0], 1 - 2 * side)
            span = slice(side * QUARTER, (side + 1) * QUARTER)
            part[axis][index, low:high, :, span] = (
                part[axis][index, low:high, :, span].astype(F32)
                + far_in[axis][side, low:high].astype(F32)
            ).astype(BF16)
            hop(axis, sub, side, True, side).start()

    def final(axis, sub):
        first, second = place[axis]
        low, high = SPANS[sub]
        arrived(near_in[axis].at[:, span_of(sub)], near_recv.at[axis, sub])
        total = own[axis][low:high]
        for side in (0, 1):
            total = total + near_in[axis][side, low:high].astype(F32)
        own[axis][low:high] = total
        send[axis][low:high] = total.astype(BF16)
        for holder in range(low, high):

            @pl.when(second != holder)
            def _():
                remote(
                    send[axis].at[holder],
                    last[axis].at[turn(second, -holder) - 1],
                    last_send,
                    last_recv.at[axis],
                    (g, member(first, holder, axis)),
                ).start()

    for axis in (0, 1):
        index = turn(place[axis][0], 2)
        part[axis][index] = product(axis, index).astype(BF16)
        for sub in range(SUBS):
            far(axis, sub)
    for axis in (0, 1):
        for side in (0, 1):
            index = turn(place[axis][0], 1 - 2 * side)
            part[axis][index] = product(axis, index).astype(BF16)
        for sub in range(SUBS):
            direct(axis, sub)
    for axis in (0, 1):
        own[axis][...] = product(axis, place[axis][0])

    lanes = iota((SHARD, BLK), 1)
    diagonal = lanes == iota((SHARD, BLK), 0)

    def total1(k):
        to = turn(z, k)
        return remote(tot1.at[to], tot1rx.at[k], tot_sem.at[0], tot_sem.at[1], (g, to * 4 + y))

    def total2(k):
        to = turn(y, k)
        return remote(tot2.at[to], tot2rx.at[k], tot_sem.at[2], tot_sem.at[3], (g, z * 4 + to))

    def total_of(i, carry):
        for j in range(4):
            found = early[4 * i + j] + lane_sums(4 * i + j, EARLY, GROUPS)
            column = jnp.sum(found, axis=1, keepdims=True)
            row = jnp.sum(jnp.where(diagonal, column, 0.0), axis=0, keepdims=True)
            tot1[i, j] = jnp.broadcast_to(row, (8, BLK))
        return carry

    lax.fori_loop(0, 4, total_of, 0)

    for axis in (0, 1):
        relay(axis, 0)
    for axis in (0, 1):
        relay(axis, 1)
    for k in range(1, 4):
        total1(k).start()
    for axis in (0, 1):
        relay(axis, 2)
    affinity = jnp.zeros((1, ROWS), F32)
    square_eye = iota((SLOTS, SLOTS), 0) == iota((SLOTS, SLOTS), 1)
    arrived(affrx.at[1:GROUPS], aff_sem.at[1])
    for k in range(GROUPS):
        column = jnp.sum(jnp.where(square_eye, affrx[k, 0:1], 0.0), axis=1, keepdims=True)
        here = slot == (slot_ids + group_at(k) * SLOTS).astype(F32)
        affinity = affinity + jnp.sum(jnp.where(here, column, 0.0), axis=0, keepdims=True)
    aff_ref[...] = affinity.reshape(ROWS)

    for axis in (0, 1):
        final(axis, 0)
    arrived(tot1rx.at[1:4], tot_sem.at[1])
    totals = tot1[z]
    for k in range(1, 4):
        totals = totals + tot1rx[k]
    tot2[...] = totals
    for k in range(1, 4):
        total2(k).start()
    for axis in (0, 1):
        final(axis, 1)
    for axis in (0, 1):
        final(axis, 2)

    totals = tot2[y]
    arrived(tot2rx.at[1:4], tot_sem.at[3])
    for k in range(1, 4):
        totals = totals + tot2rx[k]
    column = jnp.sum(jnp.where(diagonal, totals[0:1], 0.0), axis=1, keepdims=True) + PRIOR_WEIGHT
    scale = 1.0 / column

    for axis in (0, 1):
        second = place[axis][1]
        span = slice(axis * HALF, (axis + 1) * HALF)
        total = own[axis][second] + PRIOR_WEIGHT * pool[d, :, span].astype(F32)
        arrived(last[axis], last_recv.at[axis])
        for k in range(3):
            total = total + last[axis][k].astype(F32)
        new_ref[:, span] = total * scale

    left(tx.at[1:GROUPS], row_send)
    left(txf.at[1:GROUPS], flag_sem.at[0])
    left(afftx.at[1:GROUPS], aff_sem.at[0])
    left(tot1.at[0:3], tot_sem.at[0])
    left(tot2.at[0:3], tot_sem.at[2])
    left(pool.at[0:15], ag_send)
    left(weights.at[0:12], part_send)
    left(pool.at[0:3], last_send)


def local(points, coarse, candidates, centroids):
    operands = (candidates.T, points, coarse.reshape(1, ROWS), centroids)
    vmem = pl.BlockSpec(memory_space=pltpu.VMEM)
    anywhere = pl.BlockSpec(memory_space=pl.ANY)
    dma = pltpu.SemaphoreType.DMA
    updated, affinity = pl.pallas_call(
        kernel,
        out_shape=(
            jax.ShapeDtypeStruct((SHARD, WIDTH), F32),
            jax.ShapeDtypeStruct((ROWS,), F32),
        ),
        in_specs=[anywhere] * 4,
        out_specs=(vmem, vmem),
        scratch_shapes=[
            pltpu.SMEM((LISTED, CLUSTERS), jnp.int32),
            pltpu.VMEM((ROWS, WIDTH), BF16),
            pltpu.VMEM((1, ROWS), jnp.int32),
            pltpu.VMEM((GROUPS, SLOTS, WIDTH), BF16),
            pltpu.VMEM((GROUPS, SLOTS, WIDTH), BF16),
            pltpu.VMEM((GROUPS, 8, SLOTS), F32),
            pltpu.VMEM((GROUPS, 8, SLOTS), F32),
            pltpu.VMEM((MEMBERS, SHARD, WIDTH), BF16),
            pltpu.VMEM((8, BLK, SLOTS), F32),
            pltpu.VMEM((4, 4 * SHARD, 2 * SLOTS), F32),
            pltpu.VMEM((MEMBERS, SHARD, GROUPS * SLOTS), BF16),
            pltpu.VMEM((GROUPS, 8, SLOTS), F32),
            pltpu.VMEM((GROUPS, 8, SLOTS), F32),
            pltpu.VMEM((4, 4, 8, BLK), F32),
            pltpu.VMEM((4, 4, 8, BLK), F32),
            pltpu.VMEM((4, 8, BLK), F32),
            pltpu.VMEM((4, 8, BLK), F32),
            pltpu.VMEM((4, 4, SHARD, HALF), BF16),
            pltpu.VMEM((4, 4, SHARD, HALF), BF16),
            pltpu.VMEM((4, 4, SHARD, HALF), F32),
            pltpu.VMEM((4, 4, SHARD, HALF), F32),
            pltpu.VMEM((MEMBERS, SHARD, BLK), F32),
            pltpu.VMEM((4, SHARD, HALF), F32),
            pltpu.VMEM((4, SHARD, HALF), F32),
            pltpu.VMEM((2, 4, SHARD, QUARTER), BF16),
            pltpu.VMEM((2, 4, SHARD, QUARTER), BF16),
            pltpu.VMEM((2, 4, SHARD, HALF), BF16),
            pltpu.VMEM((2, 4, SHARD, HALF), BF16),
            pltpu.VMEM((4, SHARD, HALF), BF16),
            pltpu.VMEM((4, SHARD, HALF), BF16),
            pltpu.VMEM((3, SHARD, HALF), BF16),
            pltpu.VMEM((3, SHARD, HALF), BF16),
            dma((4,)),
            dma,
            dma((len(BATCHES) + 1,)),
            dma((2,)),
            dma((2,)),
            dma((4,)),
            dma,
            dma((2, 3)),
            dma,
            dma,
            dma((2, SUBS)),
            dma((2, SUBS)),
            dma,
            dma((2,)),
        ],
        compiler_params=pltpu.CompilerParams(
            collective_id=0, has_side_effects=True, vmem_limit_bytes=32 << 20
        ),
    )(*(pltpu.with_memory_space_constraint(a, pltpu.HBM) for a in operands))
    return updated, affinity


def solution(mesh):
    return jax.shard_map(
        local,
        mesh=mesh,
        in_specs=(P(("grp", "dev"), None), P(("grp", "dev"), None), P(), P(("grp", "dev"), None)),
        out_specs=(P(("grp", "dev"), None), P(("grp", "dev"))),
        check_vma=False,
    )
```
